256 devices in a mesh: mp: 32 (over x, z_lo, core), dp: 8 (over y, z_hi).
Axes of the slice: x: 4, y: 4, z: 8 (z_hi: 2, z_lo: 4; z = z_hi * 4 + z_lo), core: 2. Of those that a mesh axis runs over, the one named last changes fastest.
Arguments:
- inputs: bfloat16 [2048, 4096], P('dp', 'mp'), may hold values from -6 to 6
- qkv_weight: bfloat16 [4096, 3, 4096], P('dp', None, 'mp'), may hold values from -0.09375 to 0.09375
- out_weight: bfloat16 [4096, 4096], P('mp', 'dp'), may hold values from -0.09375 to 0.09375
- up_weight: bfloat16 [4096, 12288], P('dp', 'mp'), may hold values from -0.09375 to 0.09375
- down_weight: bfloat16 [12288, 4096], P('mp', 'dp'), may hold values from -0.0546875 to 0.0546875
- grad_out: bfloat16 [2048, 4096], P('dp', 'mp'), may hold values from -6 to 6
Outputs:
- layer_out: bfloat16 [2048, 4096], P('dp', 'mp')
- qkv_grad: bfloat16 [4096, 3, 4096], P('dp', None, 'mp')
- out_grad: bfloat16 [4096, 4096], P('mp', 'dp')
- up_grad: bfloat16 [4096, 12288], P('dp', 'mp')
- down_grad: bfloat16 [12288, 4096], P('mp', 'dp')
The draws below stay inside these ranges and needn't reach their ends.
All inputs are finite; a program needn't handle non-finite values.
Results may differ from the reference program's by a relative error of at most 0.018.
Values may be sent and summed in bfloat16 or wider, within the bound.
A program may use at most 64 MiB of HBM per device.

```python
import math
import jax
import jax.numpy as jnp
from jax import lax

D = 4096
HEADS = 32
HEAD_DIM = 128
FF = 12288
PATCHES = 256
TOK_DEV = 256
TOKENS = 2048
N_DP = 8


def shard_levels(key, shape, shards, low, high):
    gain = 1.0
    for position, shards_of in shards:
        heights = jax.random.uniform(jax.random.fold_in(jax.random.fold_in(key, 6), position), (shards_of,), jnp.float32, low / len(shards), high / len(shards))
        gain = gain * jnp.repeat(jnp.exp(heights), shape[position] // shards_of).reshape((-1,) + (1,) * (len(shape) - 1 - position))
    return gain


def scatter_about(own_key, shape, spread, limit, cuts=(), kind=jnp.bfloat16):
    drawn = spread * jax.random.normal(own_key, shape, jnp.float32)
    if cuts:
        drawn = drawn * shard_levels(own_key, shape, cuts, -0.22, 0.18)
    return jnp.clip(drawn, -limit, limit).astype(kind)


def setup_inputs(seed: int = 0) -> dict:
    streams_of = jax.random.split(jax.random.key(seed), 7)
    inputs = scatter_about(streams_of[0], (TOKENS, D), 1.0, 6.0, ((0, 8), (1, 32)))
    qkv_weight = scatter_about(streams_of[1], (D, 3, HEADS * HEAD_DIM), D ** -0.5, 0.09375, ((0, 8), (2, 32)))
    out_weight = scatter_about(streams_of[2], (HEADS * HEAD_DIM, D), (HEADS * HEAD_DIM) ** -0.5, 0.09375, ((0, 32), (1, 8)))
    up_weight = scatter_about(streams_of[3], (D, FF), D ** -0.5, 0.09375, ((0, 8), (1, 32)))
    down_weight = scatter_about(streams_of[4], (FF, D), FF ** -0.5, 0.0546875, ((0, 32), (1, 8)))
    grad_out = scatter_about(streams_of[5], (TOKENS, D), 1.0, 6.0, ((0, 8), (1, 32)))
    return {"inputs": inputs, "qkv_weight": qkv_weight, "out_weight": out_weight, "up_weight": up_weight, "down_weight": down_weight, "grad_out": grad_out}


def normalize(values):
    centre = values - lax.optimization_barrier(jnp.mean(values, axis=-1, keepdims=True))
    scale_inv = 1.0 / jnp.sqrt(lax.optimization_barrier(jnp.mean(centre * centre, axis=-1, keepdims=True)) + 1e-06)
    return (centre * scale_inv, scale_inv)

def norm_back(normed_hat, scale_inv, upstream):
    first = lax.optimization_barrier(jnp.mean(upstream, axis=-1, keepdims=True))
    second = lax.optimization_barrier(jnp.mean(upstream * normed_hat, axis=-1, keepdims=True))
    return scale_inv * (upstream - first - normed_hat * second)

def gelu_value(upper):
    return 0.5 * upper * (1.0 + lax.erf(upper * (1.0 / math.sqrt(2.0))))

def gelu_slope(upper):
    return 0.5 * (1.0 + lax.erf(upper * (1.0 / math.sqrt(2.0)))) + upper * jnp.exp(-0.5 * upper * upper) * (1.0 / math.sqrt(2.0 * math.pi))

def block_pass(block_in, block_grad, qkv_weight, out_weight, up_weight, down_weight):
    width = HEADS * HEAD_DIM
    scale = HEAD_DIM ** (-0.5)
    rows = block_in.shape[0]
    images = rows // PATCHES
    block_f = block_in.astype(jnp.float32)
    normed = normalize(block_f)[0].astype(jnp.bfloat16)
    qkv = jnp.dot(normed, qkv_weight.reshape(D, 3 * width), preferred_element_type=jnp.float32)
    shape4 = (images, PATCHES, HEADS, HEAD_DIM)
    q_hat, q_inv = normalize(qkv[:, :width].reshape(shape4))
    k_hat, k_inv = normalize(qkv[:, width:2 * width].reshape(shape4))
    q_normed = q_hat.astype(jnp.bfloat16).astype(jnp.float32)
    k_normed = k_hat.astype(jnp.bfloat16).astype(jnp.float32)
    v_round = qkv[:, 2 * width:].reshape(shape4).astype(jnp.bfloat16).astype(jnp.float32)
    scores = jnp.einsum('iphd,iqhd->ihpq', q_normed, k_normed) * scale
    expo = jnp.exp(scores)
    prob = expo / lax.optimization_barrier(jnp.sum(expo, axis=-1, keepdims=True))
    prob_round = prob.astype(jnp.bfloat16).astype(jnp.float32)
    mixed = jnp.einsum('ihpq,iqhd->iphd', prob_round, v_round).reshape(rows, width).astype(jnp.bfloat16)
    attn = jnp.dot(mixed, out_weight, preferred_element_type=jnp.float32)
    upper = jnp.dot(normed, up_weight, preferred_element_type=jnp.float32)
    hidden = gelu_value(upper).astype(jnp.bfloat16)
    mlp = jnp.dot(hidden, down_weight, preferred_element_type=jnp.float32)
    result = (block_f + attn + mlp).astype(jnp.bfloat16)
    part_down = jnp.dot(hidden.T, block_grad, preferred_element_type=jnp.float32)
    part_out = jnp.dot(mixed.T, block_grad, preferred_element_type=jnp.float32)
    d_hidden = jnp.dot(block_grad, down_weight.T, preferred_element_type=jnp.float32)
    d_up = (d_hidden * gelu_slope(upper)).astype(jnp.bfloat16)
    part_up = jnp.dot(normed.T, d_up, preferred_element_type=jnp.float32)
    d_mixed = jnp.dot(block_grad, out_weight.T, preferred_element_type=jnp.float32).astype(jnp.bfloat16)
    d_mixed = d_mixed.reshape(shape4).astype(jnp.float32)
    d_prob = jnp.einsum('iphd,iqhd->ihpq', d_mixed, v_round)
    d_value = jnp.einsum('ihpq,iphd->iqhd', prob_round, d_mixed)
    d_scores = prob * (d_prob - lax.optimization_barrier(jnp.sum(prob * d_prob, axis=-1, keepdims=True))) * scale
    d_scores = d_scores.astype(jnp.bfloat16).astype(jnp.float32)
    d_qn = jnp.einsum('ihpq,iqhd->iphd', d_scores, k_normed)
    d_kn = jnp.einsum('ihpq,iphd->iqhd', d_scores, q_normed)
    d_query = norm_back(q_hat, q_inv, d_qn).reshape(rows, width)
    d_key = norm_back(k_hat, k_inv, d_kn).reshape(rows, width)
    d_qkv = jnp.concatenate([d_query, d_key, d_value.reshape(rows, width)], axis=1).astype(jnp.bfloat16)
    part_qkv = jnp.dot(normed.T, d_qkv, preferred_element_type=jnp.float32).reshape(D, 3, width)
    return (result, (part_qkv, part_out, part_up, part_down))

def reference(inputs, qkv_weight, out_weight, up_weight, down_weight, grad_out):
    blocks_in = inputs.reshape(N_DP, TOK_DEV, D)
    blocks_grad = grad_out.reshape(N_DP, TOK_DEV, D)

    def step(carry, pair):
        result, parts = block_pass(pair[0], pair[1], qkv_weight, out_weight, up_weight, down_weight)
        carry = tuple((c + p.astype(jnp.bfloat16).astype(jnp.float32) for c, p in zip(carry, parts)))
        return (carry, result)
    start = (jnp.zeros(qkv_weight.shape, jnp.float32), jnp.zeros(out_weight.shape, jnp.float32), jnp.zeros(up_weight.shape, jnp.float32), jnp.zeros(down_weight.shape, jnp.float32))
    totals, outputs = lax.scan(step, start, (blocks_in, blocks_grad))
    layer_out = outputs.reshape(TOKENS, D)
    return (layer_out, totals[0].astype(jnp.bfloat16), totals[1].astype(jnp.bfloat16), totals[2].astype(jnp.bfloat16), totals[3].astype(jnp.bfloat16))
```

```python
import math

import jax
import jax.numpy as jnp
from jax import lax
from jax.experimental import pallas as pl
from jax.experimental.pallas import tpu as pltpu
from jax.sharding import PartitionSpec as P

HEAD = 128
TOK = 256
BF = jnp.bfloat16
F32 = jnp.float32
MESH = pl.DeviceIdType.MESH


def normalize(values):
    centre = values - jnp.mean(values, axis=-1, keepdims=True)
    scale_inv = 1.0 / jnp.sqrt(jnp.mean(centre * centre, axis=-1, keepdims=True) + 1e-06)
    return centre * scale_inv, scale_inv


def norm_back(normed_hat, scale_inv, upstream):
    first = jnp.mean(upstream, axis=-1, keepdims=True)
    second = jnp.mean(upstream * normed_hat, axis=-1, keepdims=True)
    return scale_inv * (upstream - first - normed_hat * second)


def mm(a, b):
    return lax.dot_general(a, b, (((1,), (0,)), ((), ())), preferred_element_type=F32)


def mm_nt(a, b):
    return lax.dot_general(a, b, (((1,), (1,)), ((), ())), preferred_element_type=F32)


def mm_tn(a, b):
    return lax.dot_general(a, b, (((0,), (0,)), ((), ())), preferred_element_type=F32)


def merge_stats(parts, count):
    means = [p[0:1, :] for p in parts]
    mean = sum(means) / len(parts)
    square = sum(p[1:2, :] for p in parts) + count * sum((u - mean) * (u - mean) for u in means)
    return mean, square


def two_rows(first, second, rows):
    place = lax.broadcasted_iota(jnp.int32, (rows, TOK), 0)
    return jnp.where(place == 0, first, jnp.where(place == 1, second, 0.0))


class Copies:
    def __init__(self, send, recv):
        self.send, self.recv, self.used, self.all = send, recv, 0, []

    def take(self, count):
        base = self.used
        self.used += count
        return base

    def make(self, src, dst, device, index):
        return pltpu.make_async_remote_copy(
            src_ref=src,
            dst_ref=dst,
            send_sem=self.send.at[index],
            recv_sem=self.recv.at[index],
            device_id=device,
            device_id_type=MESH,
        )

    def new(self, src, dst, device):
        copy = self.make(src, dst, device, self.take(1))
        self.all.append(copy)
        return copy


N_SEMS = 128


def kernel(
    in_ref, grad_ref, wq_ref, wo_ref, wu_ref, wd_ref,
    lay_ref, gq_ref, go_ref, gu_ref, gd_ref,
    wb, xn, ga, xa, st,
    pg, pq, pu, lg, lq, lu, sg, sq, su, zg, zq, zu,
    am, ah, aq, au,
    lp, lc, s1, lx, s2, lz, s3, fin,
    acc_x, acc_b,
    send, recv, local,
):
    m = lax.axis_index("mp")
    d = lax.axis_index("dp")
    x, zl, c = m // 8, (m // 2) % 4, m % 2
    y, zh = d // 2, d % 2

    def at(x=x, zl=zl, c=c, y=y, zh=zh):
        return {"mp": (x * 4 + zl) * 2 + c, "dp": y * 2 + zh}

    sibling = at(c=1 - c)
    z_peers = [at(zl=(zl + j) % 4) for j in (1, 2, 3)]
    x_peers = [at(x=(x + j) % 4) for j in (1, 2, 3)]
    y_peers = [at(y=(y + k) % 4) for k in (1, 2, 3)]
    far = at(zh=1 - zh)
    swap = at(x=y, zl=2 * zh + zl % 2, y=x, zh=zl // 2)
    stays = jnp.logical_and(x == y, zh == zl // 2)
    moves = jnp.logical_not(stays)

    barrier = pltpu.get_barrier_semaphore()
    near = [sibling, far] + z_peers + x_peers + y_peers
    for device in near:
        pl.semaphore_signal(barrier, inc=1, device_id=device, device_id_type=MESH)

    @pl.when(moves)
    def _():
        pl.semaphore_signal(barrier, inc=1, device_id=swap, device_id_type=MESH)
        pl.semaphore_wait(barrier, len(near) + 1)

    @pl.when(stays)
    def _():
        pl.semaphore_wait(barrier, len(near))

    copies = Copies(send, recv)

    swaps = []

    def swap_start(src, dst):
        remote = copies.make(src, dst, swap, copies.take(1))
        near_copy = pltpu.make_async_copy(src, dst, local.at[len(swaps)])
        swaps.append(remote)

        @pl.when(moves)
        def _():
            remote.start()

        @pl.when(stays)
        def _():
            near_copy.start()

        def wait():
            @pl.when(moves)
            def _():
                remote.wait_recv()

            @pl.when(stays)
            def _():
                near_copy.wait()

        return wait

    def z_start(a):
        block = a.at[c, zl % 2, x * 2 + zl // 2]
        group = [copies.new(block, block, peer) for peer in z_peers]
        for copy in group:
            copy.start()
        return group

    def rows_of(a, who):
        return a.at[c, :, pl.ds(2 * who, 2)]

    def x_start(a):
        block = rows_of(a, x)
        group = [copies.new(block, block, peer) for peer in x_peers]
        for copy in group:
            copy.start()
        return group

    def core_start(a, who):
        block = rows_of(a, who)
        copy = copies.new(block, block, sibling)
        copy.start()
        return copy

    def wait_recv(group):
        for copy in group:
            copy.wait_recv()

    def x_to_core(a, group, cores):
        for j, copy in enumerate(group):
            copy.wait_recv()
            cores.append(core_start(a, (x + 3 - j) % 4))

    def tokens(a, t):
        return jnp.concatenate([a[0, 0, t], a[1, 0, t], a[0, 1, t], a[1, 1, t]], axis=1)

    g_swap = swap_start(grad_ref, ga.at[c, zl % 2, d])

    wb[0:384, :] = wd_ref[...]
    wb[384:512, :] = wo_ref[...]

    block_f = in_ref[...].astype(F32)
    mu = jnp.mean(block_f, axis=-1, keepdims=True)
    centre = block_f - mu
    square = jnp.sum(centre * centre, axis=-1, keepdims=True)
    lane = lax.broadcasted_iota(jnp.int32, (TOK, 128), 1)
    packed = jnp.where(lane == 0, mu, jnp.where(lane == 1, square, 0.0))
    st[0] = packed.T[0:8, :]
    st_core = copies.new(st.at[0], st.at[1], sibling)
    st_core.start()

    g_swap()
    g_z = z_start(ga)

    st_core.wait_recv()
    mean, square = merge_stats([st[0], st[1]], 128.0)
    st[2] = two_rows(mean, square, 8)
    st_z = [copies.new(st.at[2], st.at[3 + j], peer) for j, peer in enumerate(z_peers)]
    for copy in st_z:
        copy.start()

    wait_recv(g_z)
    g_x = x_start(ga)
    g_core = [core_start(ga, x)]

    wait_recv(st_z)
    mean, square = merge_stats([st[2 + j] for j in range(4)], 256.0)
    st[6] = two_rows(mean, square, 8)
    st_x = [copies.new(st.at[6], st.at[7 + j], peer) for j, peer in enumerate(x_peers)]
    for copy in st_x:
        copy.start()
    wait_recv(st_x)
    mean, square = merge_stats([st[6 + j] for j in range(4)], 1024.0)
    inv = 1.0 / jnp.sqrt(square / 4096.0 + 1e-06)
    columns = two_rows(mean, inv, 128).T
    xn[...] = ((block_f - columns[:, 0:1]) * columns[:, 1:2]).astype(BF)
    x_swap = swap_start(xn, xa.at[c, zl % 2, d])

    x_to_core(ga, g_x, g_core)
    x_swap()
    x_z = z_start(xa)
    wait_recv(g_core)

    def product_start(p, land, product):
        base = copies.take(6)

        def turn(i):
            last = i // 6
            k = (i % 3 + 1) * (1 - last)
            own = (i // 3) * (1 - last) + (i - 6) * last
            to_zh = (1 - zh) * (1 - own) + zh * own
            return k, own, ((y + k) % 4) * 2 + to_zh

        def step(i, carry):
            k, own, t = turn(i)
            p[t] = product(t).astype(BF)

            @pl.when(i < 6)
            def _():
                copies.make(
                    p.at[t], land.at[own, k - 1], at(y=(y + k) % 4), base + i
                ).start()

            return carry

        lax.fori_loop(0, 8, step, 0)
        group = []
        for i in range(6):
            k, own = i % 3 + 1, i // 3
            to_zh = zh if own else 1 - zh
            t = ((y + k) % 4) * 2 + to_zh
            group.append(copies.make(p.at[t], land.at[own, k - 1], y_peers[k - 1], base + i))
        copies.all.extend(group)
        return group

    g_y = product_start(pg, lg, lambda t: mm_nt(tokens(ga, t), wb[...]))

    wait_recv(x_z)
    x_x = x_start(xa)
    x_core = [core_start(xa, x)]
    x_to_core(xa, x_x, x_core)
    wait_recv(x_core)
    q_y = product_start(pq, lq, lambda t: mm(tokens(xa, t), wq_ref[...]))
    u_y = product_start(pu, lu, lambda t: mm(tokens(xa, t), wu_ref[...]))

    mine = d
    theirs = y * 2 + 1 - zh

    def total(p, land, own, t):
        out = p[t].astype(F32)
        for k in range(3):
            out = out + land[own, k].astype(F32)
        return out

    def far_start(group, p, land, s, z):
        wait_recv(group[:3])
        s[...] = total(p, land, 0, theirs).astype(BF)
        copy = copies.new(s, z, far)
        copy.start()
        return copy

    def finish(group, copy, p, land, z):
        wait_recv(group[3:])
        copy.wait_recv()
        return total(p, land, 1, mine) + z[...].astype(F32)

    g_far = far_start(g_y, pg, lg, sg, zg)
    q_far = far_start(q_y, pq, lq, sq, zq)
    d_both = finish(g_y, g_far, pg, lg, zg)
    sg_hidden = d_both[:, :384]
    d_mixed = d_both[:, 384:].astype(BF)

    qkv = finish(q_y, q_far, pq, lq, zq)
    u_far = far_start(u_y, pu, lu, su, zu)

    scale = HEAD ** (-0.5)
    q_hat, q_inv = normalize(qkv[:, :128])
    k_hat, k_inv = normalize(qkv[:, 128:256])
    q_n = q_hat.astype(BF)
    k_n = k_hat.astype(BF)
    v_n = qkv[:, 256:].astype(BF)
    expo = jnp.exp(mm_nt(q_n, k_n) * scale)
    prob = expo / jnp.sum(expo, axis=-1, keepdims=True)
    prob_n = prob.astype(BF)
    am[mine] = mm(prob_n, v_n).astype(BF)

    def gather_far(a):
        copy = copies.new(a.at[mine], a.at[mine], far)
        copy.start()
        return copy

    def gather_y(a, t):
        group = [copies.new(a.at[t], a.at[t], peer) for peer in y_peers]
        for copy in group:
            copy.start()
        return group

    m_far = gather_far(am)
    m_y = gather_y(am, mine)

    d_prob = mm_nt(d_mixed, v_n)
    d_v = mm_tn(prob_n, d_mixed)
    d_scores = prob * (d_prob - jnp.sum(prob * d_prob, axis=-1, keepdims=True)) * scale
    d_scores = d_scores.astype(BF)
    d_q = norm_back(q_hat, q_inv, mm(d_scores, k_n))
    d_k = norm_back(k_hat, k_inv, mm_tn(d_scores, q_n))
    aq[mine] = jnp.concatenate([d_q, d_k, d_v], axis=1).astype(BF)
    q_gfar = gather_far(aq)

    upper = finish(u_y, u_far, pu, lu, zu)
    erf1 = 1.0 + lax.erf(upper * (1.0 / math.sqrt(2.0)))
    ah[mine] = (0.5 * upper * erf1).astype(BF)
    h_far = gather_far(ah)
    h_y = gather_y(ah, mine)
    slope = 0.5 * erf1 + upper * jnp.exp(-0.5 * upper * upper) * (1.0 / math.sqrt(2.0 * math.pi))
    au[mine] = (sg_hidden * slope).astype(BF)
    u_gfar = gather_far(au)
    m_far.wait_recv()
    m_y2 = gather_y(am, theirs)
    q_gy = gather_y(aq, mine)
    h_far.wait_recv()
    h_y2 = gather_y(ah, theirs)
    q_gfar.wait_recv()
    q_gy2 = gather_y(aq, theirs)
    u_gy = gather_y(au, mine)
    u_gfar.wait_recv()
    u_gy2 = gather_y(au, theirs)

    cores = []
    for k in range(4):
        if k:
            wait_recv([m_y[k - 1], m_y2[k - 1], h_y[k - 1], h_y2[k - 1]])
        g = (y + 4 - k) % 4

        def out_step(i, carry, g=g):
            t = 2 * g + i
            out = mm(jnp.concatenate([ah[t], am[t]], axis=1), wb[...]).astype(BF)
            for cb in range(4):
                lp[cb % 2, cb // 2, t] = out[:, cb * 128 : cb * 128 + 128]
            return carry

        lax.fori_loop(0, 2, out_step, 0)
        copy = copies.new(lp.at[1 - c, :, pl.ds(2 * g, 2)], lc.at[:, pl.ds(2 * g, 2)], sibling)
        copy.start()
        cores.append(copy)
    wait_recv(cores)

    def core_step(t, carry):
        for b in range(2):
            s1[b, t] = (lp[c, b, t].astype(F32) + lc[b, t].astype(F32)).astype(BF)
        return carry

    lax.fori_loop(0, 8, core_step, 0)
    o_x = []
    for j, peer in enumerate(x_peers):
        copy = copies.new(s1.at[:, pl.ds(2 * ((x + j + 1) % 4), 2)], lx.at[j], peer)
        copy.start()
        o_x.append(copy)

    acc_b[...] = jnp.zeros_like(acc_b)

    def grad_b(t, carry):
        acc_b[...] += mm_tn(jnp.concatenate([ah[t], am[t]], axis=1), tokens(ga, t))
        return carry

    lax.fori_loop(0, 8, grad_b, 0)

    wait_recv(o_x)
    for b in range(2):
        for i in range(2):
            out = s1[b, 2 * x + i].astype(F32)
            for j in range(3):
                out = out + lx[j, b, i].astype(F32)
            s2[b, i] = out.astype(BF)
    o_z = []
    for j, peer in enumerate(z_peers):
        to = (zl + j + 1) % 4
        copy = copies.new(s2.at[to % 2, to // 2], lz.at[j], peer)
        copy.start()
        o_z.append(copy)

    gd_ref[...] = acc_b[0:384, :].astype(BF)
    go_ref[...] = acc_b[384:512, :].astype(BF)
    acc_x[...] = jnp.zeros_like(acc_x)

    def grad_x(g):
        def step(i, carry):
            t = 2 * g + i
            acc_x[...] += mm_tn(tokens(xa, t), jnp.concatenate([aq[t], au[t]], axis=1))
            return carry

        lax.fori_loop(0, 2, step, 0)

    grad_x(y)
    wait_recv(o_z)
    out = s2[zl % 2, zl // 2].astype(F32)
    for j in range(3):
        out = out + lz[j].astype(F32)
    s3[...] = out.astype(BF)
    o_swap = swap_start(s3, fin)
    for k in (1, 2, 3):
        wait_recv([q_gy[k - 1], q_gy2[k - 1], u_gy[k - 1], u_gy2[k - 1]])
        grad_x((y + 4 - k) % 4)
    gq_ref[...] = acc_x[:, 0:384].astype(BF)
    gu_ref[...] = acc_x[:, 384:768].astype(BF)
    o_swap()
    lay_ref[...] = (block_f + fin[...].astype(F32)).astype(BF)

    for copy in copies.all:
        copy.wait_send()

    @pl.when(moves)
    def _():
        for copy in swaps:
            copy.wait_send()


def shards(inputs, qkv_weight, out_weight, up_weight, down_weight, grad_out):
    rows = qkv_weight.shape[0]
    vmem = pl.BlockSpec(memory_space=pltpu.VMEM)

    def buf(*shape, dtype=BF):
        return pltpu.VMEM(shape, dtype)

    layer_out, qkv_grad, out_grad, up_grad, down_grad = pl.pallas_call(
        kernel,
        out_shape=[
            jax.ShapeDtypeStruct(inputs.shape, BF),
            jax.ShapeDtypeStruct((rows, 384), BF),
            jax.ShapeDtypeStruct(out_weight.shape, BF),
            jax.ShapeDtypeStruct(up_weight.shape, BF),
            jax.ShapeDtypeStruct(down_weight.shape, BF),
        ],
        in_specs=[vmem] * 6,
        out_specs=[vmem] * 5,
        scratch_shapes=[
            buf(512, 512),
            buf(TOK, 128),
            buf(2, 2, 8, TOK, 128),
            buf(2, 2, 8, TOK, 128),
            buf(10, 8, TOK, dtype=F32),
            buf(8, TOK, 512),
            buf(8, TOK, 384),
            buf(8, TOK, 384),
            buf(2, 3, TOK, 512),
            buf(2, 3, TOK, 384),
            buf(2, 3, TOK, 384),
            buf(TOK, 512),
            buf(TOK, 384),
            buf(TOK, 384),
            buf(TOK, 512),
            buf(TOK, 384),
            buf(TOK, 384),
            buf(8, TOK, 128),
            buf(8, TOK, 384),
            buf(8, TOK, 384),
            buf(8, TOK, 384),
            buf(2, 2, 8, TOK, 128),
            buf(2, 8, TOK, 128),
            buf(2, 8, TOK, 128),
            buf(3, 2, 2, TOK, 128),
            buf(2, 2, TOK, 128),
            buf(3, TOK, 128),
            buf(TOK, 128),
            buf(TOK, 128),
            buf(512, 768, dtype=F32),
            buf(512, 512, dtype=F32),
            pltpu.SemaphoreType.DMA((N_SEMS,)),
            pltpu.SemaphoreType.DMA((N_SEMS,)),
            pltpu.SemaphoreType.DMA((4,)),
        ],
        compiler_params=pltpu.CompilerParams(
            collective_id=0, has_side_effects=True, vmem_limit_bytes=56 * 2**20
        ),
    )(inputs, grad_out, qkv_weight.reshape(rows, 384), out_weight, up_weight, down_weight)
    return layer_out, qkv_grad.reshape(qkv_weight.shape), out_grad, up_grad, down_grad


def solution(mesh):
    placed = (
        P("dp", "mp"),
        P("dp", None, "mp"),
        P("mp", "dp"),
        P("dp", "mp"),
        P("mp", "dp"),
        P("dp", "mp"),
    )
    return jax.shard_map(
        shards,
        mesh=mesh,
        in_specs=placed,
        out_specs=(P("dp", "mp"), P("dp", None, "mp"), P("mp", "dp"), P("dp", "mp"), P("mp", "dp")),
        check_vma=False,
    )
```

```python
import math

import jax
import jax.numpy as jnp
from jax import lax
from jax.experimental import pallas as pl
from jax.experimental.pallas import tpu as pltpu
from jax.sharding import PartitionSpec as P

HEAD = 128
TOK = 256
BF = jnp.bfloat16
F32 = jnp.float32
MESH = pl.DeviceIdType.MESH


def normalize(values):
    centre = values - jnp.mean(values, axis=-1, keepdims=True)
    scale_inv = 1.0 / jnp.sqrt(jnp.mean(centre * centre, axis=-1, keepdims=True) + 1e-06)
    return centre * scale_inv, scale_inv


def norm_back(normed_hat, scale_inv, upstream):
    first = jnp.mean(upstream, axis=-1, keepdims=True)
    second = jnp.mean(upstream * normed_hat, axis=-1, keepdims=True)
    return scale_inv * (upstream - first - normed_hat * second)


def mm(a, b):
    return lax.dot_general(a, b, (((1,), (0,)), ((), ())), preferred_element_type=F32)


def mm_nt(a, b):
    return lax.dot_general(a, b, (((1,), (1,)), ((), ())), preferred_element_type=F32)


def mm_tn(a, b):
    return lax.dot_general(a, b, (((0,), (0,)), ((), ())), preferred_element_type=F32)


def merge_stats(parts, count):
    means = [p[0:1, :] for p in parts]
    mean = sum(means) / len(parts)
    square = sum(p[1:2, :] for p in parts) + count * sum((u - mean) * (u - mean) for u in means)
    return mean, square


def two_rows(first, second, rows):
    place = lax.broadcasted_iota(jnp.int32, (rows, TOK), 0)
    return jnp.where(place == 0, first, jnp.where(place == 1, second, 0.0))


class Copies:
    def __init__(self, send, recv):
        self.send, self.recv, self.used, self.all = send, recv, 0, []

    def take(self, count):
        base = self.used
        self.used += count
        return base

    def make(self, src, dst, device, index):
        return pltpu.make_async_remote_copy(
            src_ref=src,
            dst_ref=dst,
            send_sem=self.send.at[index],
            recv_sem=self.recv.at[index],
            device_id=device,
            device_id_type=MESH,
        )

    def new(self, src, dst, device):
        copy = self.make(src, dst, device, self.take(1))
        self.all.append(copy)
        return copy


N_SEMS = 192


def kernel(
    in_ref, grad_ref, wq_ref, wo_ref, wu_ref, wd_ref,
    lay_ref, gq_ref, go_ref, gu_ref, gd_ref,
    wb, wq, sa, xb, ga, xa, st,
    pg, pq, pu, lg, lq, lu, rg, rq, ru, sg, sq, su, zg, zq, zu,
    am, ah, aq, au,
    lp, lc, s1, lx, s2, lz, s3, fin,
    acc_x, acc_b,
    send, recv, local,
):
    m = lax.axis_index("mp")
    d = lax.axis_index("dp")
    x, zl, c = m // 8, (m // 2) % 4, m % 2
    y, zh = d // 2, d % 2

    def at(x=x, zl=zl, c=c, y=y, zh=zh):
        return {"mp": (x * 4 + zl) * 2 + c, "dp": y * 2 + zh}

    sibling = at(c=1 - c)
    z_peers = [at(zl=(zl + j) % 4) for j in (1, 2, 3)]
    x_peers = [at(x=(x + j) % 4) for j in (1, 2, 3)]
    y_peers = [at(y=(y + k) % 4) for k in (1, 2, 3)]
    y_up, y_down = y_peers[0], y_peers[2]
    far = at(zh=1 - zh)
    swap = at(x=y, zl=2 * zh + zl % 2, y=x, zh=zl // 2)
    stays = jnp.logical_and(x == y, zh == zl // 2)
    moves = jnp.logical_not(stays)

    barrier = pltpu.get_barrier_semaphore()
    near = [sibling, far] + z_peers + x_peers + y_peers
    for device in near:
        pl.semaphore_signal(barrier, inc=1, device_id=device, device_id_type=MESH)

    @pl.when(moves)
    def _():
        pl.semaphore_signal(barrier, inc=1, device_id=swap, device_id_type=MESH)

    block_f = in_ref[...].astype(F32)
    mu = jnp.mean(block_f, axis=-1, keepdims=True)
    centre = block_f - mu
    square = jnp.sum(centre * centre, axis=-1, keepdims=True)
    lane = lax.broadcasted_iota(jnp.int32, (TOK, 128), 1)
    packed = jnp.where(lane == 0, mu, jnp.where(lane == 1, square, 0.0))
    st[0] = packed.T[0:8, :]
    wb[0:384, :] = wd_ref[...]
    wb[384:512, :] = wo_ref[...]
    for i in range(3):
        wq[:, i * 128 : i * 128 + 128] = wq_ref[i]

    @pl.when(moves)
    def _():
        pl.semaphore_wait(barrier, len(near) + 1)

    @pl.when(stays)
    def _():
        pl.semaphore_wait(barrier, len(near))

    copies = Copies(send, recv)
    swaps = []

    def swap_start(src, dst):
        remote = copies.make(src, dst, swap, copies.take(1))
        near_copy = pltpu.make_async_copy(src, dst, local.at[len(swaps)])
        swaps.append(remote)

        @pl.when(moves)
        def _():
            remote.start()

        @pl.when(stays)
        def _():
            near_copy.start()

        def wait():
            @pl.when(moves)
            def _():
                remote.wait_recv()

            @pl.when(stays)
            def _():
                near_copy.wait()

        return wait

    def send_all(block, peers):
        group = [copies.new(block, block, peer) for peer in peers]
        for copy in group:
            copy.start()
        return group

    def z_start(a):
        return send_all(a.at[c, zl % 2, x * 2 + zl // 2], z_peers)

    def half_of(a, who, half):
        return a.at[c, half, pl.ds(2 * who, 2)]

    def to_core(a, who):
        return send_all(a.at[c, :, pl.ds(2 * who, 2)], [sibling])

    def x_start(a):
        up = [copies.new(h, h, x_peers[0]) for h in (half_of(a, x, 0), half_of(a, x, 1))]
        down = [copies.new(h, h, x_peers[2]) for h in (half_of(a, x, 1), half_of(a, x, 0))]
        for pair in zip(up, down):
            for copy in pair:
                copy.start()
        return up, down

    def x_forward(a, group):
        up, down = group
        up[0].wait_recv()
        fars = send_all(half_of(a, x_before, 0), [x_peers[0]])
        down[0].wait_recv()
        fars += send_all(half_of(a, x_after, 1), [x_peers[2]])
        up[1].wait_recv()
        first = to_core(a, x_before)
        down[1].wait_recv()
        return fars, first, to_core(a, x_after)

    def wait_recv(group):
        for copy in group:
            copy.wait_recv()

    def tokens(a, t):
        return jnp.concatenate([a[0, 0, t], a[1, 0, t], a[0, 1, t], a[1, 1, t]], axis=1)

    x_before, x_after, x_far = (x + 3) % 4, (x + 1) % 4, (x + 2) % 4
    mine = d
    theirs = y * 2 + 1 - zh
    before, after = (y + 3) % 4, (y + 1) % 4
    low, high = pl.ds(0, TOK // 2), pl.ds(TOK // 2, TOK // 2)

    def group_plan(p, land, relay):
        out = []
        for own in range(2):
            to_zh = zh if own else 1 - zh
            t = [((y + k) % 4) * 2 + to_zh for k in range(4)]
            out.append([
                copies.new(p.at[t[2], low], relay.at[own, 0], y_up),
                copies.new(p.at[t[2], high], relay.at[own, 1], y_down),
                copies.new(p.at[t[1], high], land.at[own, 0, high], y_up),
                copies.new(p.at[t[3], low], land.at[own, 1, low], y_down),
            ])
        return out

    def group_send(out, who, owns):
        k = (who + 4 - y) % 4

        @pl.when(k == 2)
        def _():
            for own in owns:
                out[own][0].start()
                out[own][1].start()

        @pl.when(k == 1)
        def _():
            for own in owns:
                out[own][2].start()

        @pl.when(k == 3)
        def _():
            for own in owns:
                out[own][3].start()

    def products(p, product, who):
        def step(i, carry):
            t = 2 * who + i
            p[t] = product(t).astype(BF)
            return carry

        lax.fori_loop(0, 2, step, 0)

    def send_own(out, own):
        for copy in out[own][:4]:
            copy.start()

    def products_own(p, product, own):
        to_zh = zh if own else 1 - zh

        def step(i, carry):
            t = 2 * i + to_zh
            p[t] = product(t).astype(BF)
            return carry

        lax.fori_loop(0, 4, step, 0)

    def relay_on(out, p, land, relay, own):
        group = out[own]
        to_zh = zh if own else 1 - zh
        up, down = after * 2 + to_zh, before * 2 + to_zh
        group[0].wait_recv()
        p[up, low] = (p[up, low].astype(F32) + relay[own, 0].astype(F32)).astype(BF)
        copy = copies.new(p.at[up, low], land.at[own, 0, low], y_up)
        copy.start()
        group.append(copy)
        group[1].wait_recv()
        p[down, high] = (p[down, high].astype(F32) + relay[own, 1].astype(F32)).astype(BF)
        copy = copies.new(p.at[down, high], land.at[own, 1, high], y_down)
        copy.start()
        group.append(copy)

    def total(p, land, own, t):
        return p[t].astype(F32) + land[own, 0].astype(F32) + land[own, 1].astype(F32)

    def far_start(out, p, land, s, z):
        wait_recv(out[0][2:])
        s[...] = total(p, land, 0, theirs).astype(BF)
        copy = copies.new(s, z, far)
        copy.start()
        return copy

    def finish(out, copy, p, land, z):
        wait_recv(out[1][2:])
        copy.wait_recv()
        return total(p, land, 1, mine) + z[...].astype(F32)

    def gather_far(a):
        copy = copies.new(a.at[mine], a.at[mine], far)
        copy.start()
        return copy

    def gather_y(a, t):
        a0, a1 = a.at[t, low], a.at[t, high]
        group = [
            copies.new(a0, a0, y_up),
            copies.new(a1, a1, y_down),
            copies.new(a1, a1, y_up),
            copies.new(a0, a0, y_down),
        ]
        for copy in group:
            copy.start()
        return group

    def gather_relay(group, a, to_zh):
        group[0].wait_recv()
        block = a.at[before * 2 + to_zh, low]
        copy = copies.new(block, block, y_up)
        copy.start()
        group.append(copy)
        group[1].wait_recv()
        block = a.at[after * 2 + to_zh, high]
        copy = copies.new(block, block, y_down)
        copy.start()
        group.append(copy)

    def gather_wait(groups, k):
        for group in groups:
            if k == 1:
                group[2].wait_recv()
            elif k == 3:
                group[3].wait_recv()
            else:
                wait_recv(group[4:])

    g_swap = swap_start(grad_ref, ga.at[c, zl % 2, d])
    st_core = copies.new(st.at[0], st.at[1], sibling)
    st_core.start()
    x_swap = swap_start(in_ref, xa.at[c, zl % 2, d])
    st_core.wait_recv()
    mean, square = merge_stats([st[0], st[1]], 128.0)
    st[2] = two_rows(mean, square, 8)
    st_z = [copies.new(st.at[2], st.at[3 + j], peer) for j, peer in enumerate(z_peers)]
    for copy in st_z:
        copy.start()
    g_swap()
    g_z = z_start(ga)
    wait_recv(st_z)
    mean, square = merge_stats([st[2 + j] for j in range(4)], 256.0)
    st[6] = two_rows(mean, square, 8)
    st_x = [copies.new(st.at[6], st.at[7 + j], peer) for j, peer in enumerate(x_peers)]
    for copy in st_x:
        copy.start()
    x_swap()
    x_z = z_start(xa)
    wait_recv(g_z)
    g_x = x_start(ga)
    g_core = to_core(ga, x)
    wait_recv(st_x)
    mean, square = merge_stats([st[6 + j] for j in range(4)], 1024.0)
    inv = 1.0 / jnp.sqrt(square / 4096.0 + 1e-06)
    sa[mine] = two_rows(mean, inv, 8)
    st_far = send_all(sa.at[mine], [far])
    st_y = send_all(sa.at[mine], y_peers)
    g_out = group_plan(pg, lg, rg)
    u_out = group_plan(pu, lu, ru)
    q_out = group_plan(pq, lq, rq)

    def g_step(core, who):
        wait_recv(core)
        products(pg, lambda t: mm_nt(tokens(ga, t), wb[...]), who)
        group_send(g_out, who, (0, 1))

    def x_step(core, who):
        wait_recv(core)

        def step(i, carry):
            t = 2 * who + i
            columns = jnp.concatenate([sa[t], jnp.zeros((120, TOK), F32)], axis=0).T
            rows = tokens(xa, t).astype(F32)
            xb[t] = ((rows - columns[:, 0:1]) * columns[:, 1:2]).astype(BF)
            return carry

        lax.fori_loop(0, 2, step, 0)
        products(pu, lambda t: mm(xb[t], wu_ref[...]), who)
        group_send(u_out, who, (0,))

    g_step(g_core, x)
    g_fars, g_first, g_second = x_forward(ga, g_x)
    wait_recv(x_z)
    x_x = x_start(xa)
    x_core = to_core(xa, x)
    g_step(g_first, x_before)
    g_step(g_second, x_after)
    wait_recv(st_far)
    st_y2 = send_all(sa.at[theirs], y_peers)
    wait_recv(g_fars)
    g_step(to_core(ga, x_far), x_far)
    x_fars, x_first, x_second = x_forward(xa, x_x)
    relay_on(g_out, pg, lg, rg, 0)
    relay_on(g_out, pg, lg, rg, 1)
    wait_recv(st_y + st_y2)
    x_step(x_core, x)
    x_step(x_first, x_before)
    g_far = far_start(g_out, pg, lg, sg, zg)
    x_step(x_second, x_after)
    wait_recv(x_fars)
    x_step(to_core(xa, x_far), x_far)
    products_own(pq, lambda t: mm(xb[t], wq[...]), 0)
    send_own(q_out, 0)
    relay_on(u_out, pu, lu, ru, 0)
    send_own(u_out, 1)
    products_own(pq, lambda t: mm(xb[t], wq[...]), 1)
    relay_on(q_out, pq, lq, rq, 0)
    send_own(q_out, 1)
    u_far = far_start(u_out, pu, lu, su, zu)
    relay_on(u_out, pu, lu, ru, 1)
    q_far = far_start(q_out, pq, lq, sq, zq)
    relay_on(q_out, pq, lq, rq, 1)
    d_both = finish(g_out, g_far, pg, lg, zg)
    d_hidden = d_both[:, :384]
    d_mixed = d_both[:, 384:].astype(BF)
    upper = finish(u_out, u_far, pu, lu, zu)
    erf1 = 1.0 + lax.erf(upper * (1.0 / math.sqrt(2.0)))
    ah[mine] = (0.5 * upper * erf1).astype(BF)
    h_far = gather_far(ah)
    h_y = gather_y(ah, mine)
    slope = 0.5 * erf1 + upper * jnp.exp(-0.5 * upper * upper) * (1.0 / math.sqrt(2.0 * math.pi))
    au[mine] = (d_hidden * slope).astype(BF)
    u_gy = gather_y(au, mine)
    gather_relay(h_y, ah, zh)
    qkv = finish(q_out, q_far, pq, lq, zq)

    scale = HEAD ** (-0.5)
    q_hat, q_inv = normalize(qkv[:, :128])
    k_hat, k_inv = normalize(qkv[:, 128:256])
    q_n = q_hat.astype(BF)
    k_n = k_hat.astype(BF)
    v_n = qkv[:, 256:].astype(BF)
    expo = jnp.exp(mm_nt(q_n, k_n) * scale)
    prob = expo / jnp.sum(expo, axis=-1, keepdims=True)
    prob_n = prob.astype(BF)
    am[mine] = mm(prob_n, v_n).astype(BF)

    m_far = gather_far(am)
    m_y = gather_y(am, mine)
    u_gfar = gather_far(au)
    d_prob = mm_nt(d_mixed, v_n)
    d_v = mm_tn(prob_n, d_mixed)
    d_scores = prob * (d_prob - jnp.sum(prob * d_prob, axis=-1, keepdims=True)) * scale
    d_scores = d_scores.astype(BF)
    d_q = norm_back(q_hat, q_inv, mm(d_scores, k_n))
    d_k = norm_back(k_hat, k_inv, mm_tn(d_scores, q_n))
    aq[mine] = jnp.concatenate([d_q, d_k, d_v], axis=1).astype(BF)
    q_gfar = gather_far(aq)
    h_far.wait_recv()
    h_y2 = gather_y(ah, theirs)
    gather_relay(u_gy, au, zh)
    gather_relay(m_y, am, zh)
    m_far.wait_recv()
    m_y2 = gather_y(am, theirs)
    q_gy = gather_y(aq, mine)
    gather_relay(h_y2, ah, 1 - zh)
    gather_relay(m_y2, am, 1 - zh)
    u_gfar.wait_recv()
    u_gy2 = gather_y(au, theirs)
    gather_relay(q_gy, aq, zh)

    o_x = [
        copies.new(s1.at[:, pl.ds(2 * ((x + j) % 4), 2)], lx.at[j - 1], x_peers[j - 1])
        for j in (1, 2, 3)
    ]

    def out_product(k):
        if k:
            gather_wait([m_y, m_y2, h_y, h_y2], k)
        g = (y + 4 - k) % 4

        def out_step(i, carry, g=g):
            t = 2 * g + i
            out = mm(jnp.concatenate([ah[t], am[t]], axis=1), wb[...]).astype(BF)
            for cb in range(4):
                lp[cb % 2, cb // 2, t] = out[:, cb * 128 : cb * 128 + 128]
            return carry

        lax.fori_loop(0, 2, out_step, 0)
        copy = copies.new(lp.at[1 - c, :, pl.ds(2 * g, 2)], lc.at[:, pl.ds(2 * g, 2)], sibling)
        copy.start()
        return copy

    def out_core(copy, k):
        copy.wait_recv()
        g = (y + 4 - k) % 4

        def core_step(i, carry):
            t = 2 * g + i
            for b in range(2):
                s1[b, t] = (lp[c, b, t].astype(F32) + lc[b, t].astype(F32)).astype(BF)
            return carry

        lax.fori_loop(0, 2, core_step, 0)
        for j in (1, 2, 3):

            @pl.when((g + 4 - x) % 4 == j)
            def _():
                o_x[j - 1].start()

    c0 = out_product(0)
    c1 = out_product(1)
    c3 = out_product(3)
    out_core(c0, 0)
    c2 = out_product(2)
    out_core(c1, 1)
    out_core(c3, 3)
    out_core(c2, 2)
    gather_relay(u_gy2, au, 1 - zh)
    q_gfar.wait_recv()
    q_gy2 = gather_y(aq, theirs)
    acc_b[...] = jnp.zeros_like(acc_b)

    def grad_b(t, carry):
        acc_b[...] += mm_tn(jnp.concatenate([ah[t], am[t]], axis=1), tokens(ga, t))
        return carry

    lax.fori_loop(0, 8, grad_b, 0)

    gather_relay(q_gy2, aq, 1 - zh)
    wait_recv(o_x)
    for b in range(2):
        for i in range(2):
            out = s1[b, 2 * x + i].astype(F32)
            for j in range(3):
                out = out + lx[j, b, i].astype(F32)
            s2[b, i] = out.astype(BF)
    o_z = []
    for j, peer in enumerate(z_peers):
        to = (zl + j + 1) % 4
        copy = copies.new(s2.at[to % 2, to // 2], lz.at[j], peer)
        copy.start()
        o_z.append(copy)

    gd_ref[...] = acc_b[0:384, :].astype(BF)
    go_ref[...] = acc_b[384:512, :].astype(BF)
    acc_x[...] = jnp.zeros_like(acc_x)

    def grad_x(g):
        def step(i, carry):
            t = 2 * g + i
            acc_x[...] += mm_tn(xb[t], jnp.concatenate([aq[t], au[t]], axis=1))
            return carry

        lax.fori_loop(0, 2, step, 0)

    grad_x(y)
    wait_recv(o_z)
    out = s2[zl % 2, zl // 2].astype(F32)
    for j in range(3):
        out = out + lz[j].astype(F32)
    s3[...] = out.astype(BF)
    o_swap = swap_start(s3, fin)
    for k in (1, 3, 2):
        gather_wait([q_gy, q_gy2, u_gy, u_gy2], k)
        grad_x((y + 4 - k) % 4)
    for i in range(3):
        gq_ref[i] = acc_x[:, i * 128 : i * 128 + 128].astype(BF)
    gu_ref[...] = acc_x[:, 384:768].astype(BF)
    o_swap()
    lay_ref[...] = (block_f + fin[...].astype(F32)).astype(BF)

    for copy in copies.all:
        copy.wait_send()

    @pl.when(moves)
    def _():
        for copy in swaps:
            copy.wait_send()


def shards(inputs, qkv_weight, out_weight, up_weight, down_weight, grad_out):
    rows = qkv_weight.shape[0]
    vmem = pl.BlockSpec(memory_space=pltpu.VMEM)

    def buf(*shape, dtype=BF):
        return pltpu.VMEM(shape, dtype)

    layer_out, qkv_grad, out_grad, up_grad, down_grad = pl.pallas_call(
        kernel,
        out_shape=[
            jax.ShapeDtypeStruct(inputs.shape, BF),
            jax.ShapeDtypeStruct((3, rows, 128), BF),
            jax.ShapeDtypeStruct(out_weight.shape, BF),
            jax.ShapeDtypeStruct(up_weight.shape, BF),
            jax.ShapeDtypeStruct(down_weight.shape, BF),
        ],
        in_specs=[vmem] * 6,
        out_specs=[vmem] * 5,
        scratch_shapes=[
            buf(512, 512),
            buf(512, 384),
            buf(8, 8, TOK, dtype=F32),
            buf(8, TOK, 512),
            buf(2, 2, 8, TOK, 128),
            buf(2, 2, 8, TOK, 128),
            buf(10, 8, TOK, dtype=F32),
            buf(8, TOK, 512),
            buf(8, TOK, 384),
            buf(8, TOK, 384),
            buf(2, 2, TOK, 512),
            buf(2, 2, TOK, 384),
            buf(2, 2, TOK, 384),
            buf(2, 2, TOK // 2, 512),
            buf(2, 2, TOK // 2, 384),
            buf(2, 2, TOK // 2, 384),
            buf(TOK, 512),
            buf(TOK, 384),
            buf(TOK, 384),
            buf(TOK, 512),
            buf(TOK, 384),
            buf(TOK, 384),
            buf(8, TOK, 128),
            buf(8, TOK, 384),
            buf(8, TOK, 384),
            buf(8, TOK, 384),
            buf(2, 2, 8, TOK, 128),
            buf(2, 8, TOK, 128),
            buf(2, 8, TOK, 128),
            buf(3, 2, 2, TOK, 128),
            buf(2, 2, TOK, 128),
            buf(3, TOK, 128),
            buf(TOK, 128),
            buf(TOK, 128),
            buf(512, 768, dtype=F32),
            buf(512, 512, dtype=F32),
            pltpu.SemaphoreType.DMA((N_SEMS,)),
            pltpu.SemaphoreType.DMA((N_SEMS,)),
            pltpu.SemaphoreType.DMA((4,)),
        ],
        compiler_params=pltpu.CompilerParams(
            collective_id=0, has_side_effects=True, vmem_limit_bytes=56 * 2**20
        ),
    )(inputs, grad_out, jnp.transpose(qkv_weight, (1, 0, 2)), out_weight, up_weight, down_weight)
    return layer_out, jnp.transpose(qkv_grad, (1, 0, 2)), out_grad, up_grad, down_grad


def solution(mesh):
    placed = (
        P("dp", "mp"),
        P("dp", None, "mp"),
        P("mp", "dp"),
        P("dp", "mp"),
        P("mp", "dp"),
        P("dp", "mp"),
    )
    return jax.shard_map(
        shards,
        mesh=mesh,
        in_specs=placed,
        out_specs=(P("dp", "mp"), P("dp", None, "mp"), P("mp", "dp"), P("dp", "mp"), P("mp", "dp")),
        check_vma=False,
    )
```

```python
import math

import jax
import jax.numpy as jnp
from jax import lax
from jax.experimental import pallas as pl
from jax.experimental.pallas import tpu as pltpu
from jax.sharding import PartitionSpec as P

HEAD = 128
TOK = 256
BF = jnp.bfloat16
F32 = jnp.float32
MESH = pl.DeviceIdType.MESH


def normalize(values):
    centre = values - jnp.mean(values, axis=-1, keepdims=True)
    scale_inv = 1.0 / jnp.sqrt(jnp.mean(centre * centre, axis=-1, keepdims=True) + 1e-06)
    return centre * scale_inv, scale_inv


def norm_back(normed_hat, scale_inv, upstream):
    first = jnp.mean(upstream, axis=-1, keepdims=True)
    second = jnp.mean(upstream * normed_hat, axis=-1, keepdims=True)
    return scale_inv * (upstream - first - normed_hat * second)


def mm(a, b):
    return lax.dot_general(a, b, (((1,), (0,)), ((), ())), preferred_element_type=F32)


def mm_nt(a, b):
    return lax.dot_general(a, b, (((1,), (1,)), ((), ())), preferred_element_type=F32)


def mm_tn(a, b):
    return lax.dot_general(a, b, (((0,), (0,)), ((), ())), preferred_element_type=F32)


def merge_stats(parts, count):
    means = [p[0:1, :] for p in parts]
    mean = sum(means) / len(parts)
    square = sum(p[1:2, :] for p in parts) + count * sum((u - mean) * (u - mean) for u in means)
    return mean, square


def two_rows(first, second, rows):
    place = lax.broadcasted_iota(jnp.int32, (rows, TOK), 0)
    return jnp.where(place == 0, first, jnp.where(place == 1, second, 0.0))


class Copies:
    def __init__(self, send, recv):
        self.send, self.recv, self.used, self.all = send, recv, 0, []

    def take(self, count):
        base = self.used
        self.used += count
        return base

    def make(self, src, dst, device, index):
        return pltpu.make_async_remote_copy(
            src_ref=src,
            dst_ref=dst,
            send_sem=self.send.at[index],
            recv_sem=self.recv.at[index],
            device_id=device,
            device_id_type=MESH,
        )

    def new(self, src, dst, device):
        copy = self.make(src, dst, device, self.take(1))
        self.all.append(copy)
        return copy


N_SEMS = 192


def kernel(
    in_ref, grad_ref, wq_ref, wo_ref, wu_ref, wd_ref,
    lay_ref, gq_ref, go_ref, gu_ref, gd_ref,
    wb, wq, sa, xb, ga, xa, st,
    pg, pq, pu, lg, lq, lu, rg, rq, ru, sg, sq, su, zg, zq, zu,
    am, ah, aq, au,
    lp, lc, s1, lx, s2, lz, s3, fin,
    acc_x, acc_b,
    send, recv, local,
):
    m = lax.axis_index("mp")
    d = lax.axis_index("dp")
    x, zl, c = m // 8, (m // 2) % 4, m % 2
    y, zh = d // 2, d % 2

    def at(x=x, zl=zl, c=c, y=y, zh=zh):
        return {"mp": (x * 4 + zl) * 2 + c, "dp": y * 2 + zh}

    sibling = at(c=1 - c)
    z_peers = [at(zl=(zl + j) % 4) for j in (1, 2, 3)]
    x_peers = [at(x=(x + j) % 4) for j in (1, 2, 3)]
    y_peers = [at(y=(y + k) % 4) for k in (1, 2, 3)]
    y_up, y_down = y_peers[0], y_peers[2]
    far = at(zh=1 - zh)
    swap = at(x=y, zl=2 * zh + zl % 2, y=x, zh=zl // 2)
    stays = jnp.logical_and(x == y, zh == zl // 2)
    moves = jnp.logical_not(stays)

    barrier = pltpu.get_barrier_semaphore()
    near = [sibling, far] + z_peers + x_peers + y_peers
    for device in near:
        pl.semaphore_signal(barrier, inc=1, device_id=device, device_id_type=MESH)

    @pl.when(moves)
    def _():
        pl.semaphore_signal(barrier, inc=1, device_id=swap, device_id_type=MESH)

    block_f = in_ref[...].astype(F32)
    mu = jnp.mean(block_f, axis=-1, keepdims=True)
    centre = block_f - mu
    square = jnp.sum(centre * centre, axis=-1, keepdims=True)
    lane = lax.broadcasted_iota(jnp.int32, (TOK, 128), 1)
    packed = jnp.where(lane == 0, mu, jnp.where(lane == 1, square, 0.0))
    st[0] = packed.T[0:8, :]
    wb[0:384, :] = wd_ref[...]
    wb[384:512, :] = wo_ref[...]
    for i in range(3):
        wq[:, i * 128 : i * 128 + 128] = wq_ref[i]

    @pl.when(moves)
    def _():
        pl.semaphore_wait(barrier, len(near) + 1)

    @pl.when(stays)
    def _():
        pl.semaphore_wait(barrier, len(near))

    copies = Copies(send, recv)
    swaps = []

    def swap_start(src, dst):
        remote = copies.make(src, dst, swap, copies.take(1))
        near_copy = pltpu.make_async_copy(src, dst, local.at[len(swaps)])
        swaps.append(remote)

        @pl.when(moves)
        def _():
            remote.start()

        @pl.when(stays)
        def _():
            near_copy.start()

        def wait():
            @pl.when(moves)
            def _():
                remote.wait_recv()

            @pl.when(stays)
            def _():
                near_copy.wait()

        return wait

    def send_all(block, peers):
        group = [copies.new(block, block, peer) for peer in peers]
        for copy in group:
            copy.start()
        return group

    def z_start(a):
        return send_all(a.at[c, zl % 2, x * 2 + zl // 2], z_peers)

    def half_of(a, who, half):
        return a.at[c, half, pl.ds(2 * who, 2)]

    def to_core(a, who):
        return send_all(a.at[c, :, pl.ds(2 * who, 2)], [sibling])

    def x_start(a):
        up = [copies.new(h, h, x_peers[0]) for h in (half_of(a, x, 0), half_of(a, x, 1))]
        down = [copies.new(h, h, x_peers[2]) for h in (half_of(a, x, 1), half_of(a, x, 0))]
        for pair in zip(up, down):
            for copy in pair:
                copy.start()
        return up, down

    def x_forward(a, group):
        up, down = group
        up[0].wait_recv()
        fars = send_all(half_of(a, x_before, 0), [x_peers[0]])
        down[0].wait_recv()
        fars += send_all(half_of(a, x_after, 1), [x_peers[2]])
        up[1].wait_recv()
        first = to_core(a, x_before)
        down[1].wait_recv()
        return fars, first, to_core(a, x_after)

    def wait_recv(group):
        for copy in group:
            copy.wait_recv()

    def tokens(a, t):
        return jnp.concatenate([a[0, 0, t], a[1, 0, t], a[0, 1, t], a[1, 1, t]], axis=1)

    x_before, x_after, x_far = (x + 3) % 4, (x + 1) % 4, (x + 2) % 4
    mine = d
    theirs = y * 2 + 1 - zh
    before, after = (y + 3) % 4, (y + 1) % 4
    low, high = pl.ds(0, TOK // 2), pl.ds(TOK // 2, TOK // 2)

    def group_plan(p, land, relay):
        out = []
        for own in range(2):
            to_zh = zh if own else 1 - zh
            t = [((y + k) % 4) * 2 + to_zh for k in range(4)]
            out.append([
                copies.new(p.at[t[2], low], relay.at[own, 0], y_up),
                copies.new(p.at[t[2], high], relay.at[own, 1], y_down),
                copies.new(p.at[t[1], high], land.at[own, 0, high], y_up),
                copies.new(p.at[t[3], low], land.at[own, 1, low], y_down),
            ])
        return out

    def group_send(out, who, owns):
        k = (who + 4 - y) % 4

        @pl.when(k == 2)
        def _():
            for own in owns:
                out[own][0].start()
                out[own][1].start()

        @pl.when(k == 1)
        def _():
            for own in owns:
                out[own][2].start()

        @pl.when(k == 3)
        def _():
            for own in owns:
                out[own][3].start()

    def products(p, product, who):
        def step(i, carry):
            t = 2 * who + i
            p[t] = product(t).astype(BF)
            return carry

        lax.fori_loop(0, 2, step, 0)

    def send_own(out, own):
        for copy in out[own][:4]:
            copy.start()

    def products_own(p, product, own):
        to_zh = zh if own else 1 - zh

        def step(i, carry):
            t = 2 * i + to_zh
            p[t] = product(t).astype(BF)
            return carry

        lax.fori_loop(0, 4, step, 0)

    def relay_on(out, p, land, relay, own):
        group = out[own]
        to_zh = zh if own else 1 - zh
        up, down = after * 2 + to_zh, before * 2 + to_zh
        group[0].wait_recv()
        p[up, low] = (p[up, low].astype(F32) + relay[own, 0].astype(F32)).astype(BF)
        copy = copies.new(p.at[up, low], land.at[own, 0, low], y_up)
        copy.start()
        group.append(copy)
        group[1].wait_recv()
        p[down, high] = (p[down, high].astype(F32) + relay[own, 1].astype(F32)).astype(BF)
        copy = copies.new(p.at[down, high], land.at[own, 1, high], y_down)
        copy.start()
        group.append(copy)

    def total(p, land, own, t):
        return p[t].astype(F32) + land[own, 0].astype(F32) + land[own, 1].astype(F32)

    def far_start(out, p, land, s, z):
        wait_recv(out[0][2:])
        s[...] = total(p, land, 0, theirs).astype(BF)
        copy = copies.new(s, z, far)
        copy.start()
        return copy

    def finish(out, copy, p, land, z):
        wait_recv(out[1][2:])
        copy.wait_recv()
        return total(p, land, 1, mine) + z[...].astype(F32)

    def gather_far(a):
        copy = copies.new(a.at[mine], a.at[mine], far)
        copy.start()
        return copy

    def gather_y(a, t):
        a0, a1 = a.at[t, low], a.at[t, high]
        group = [
            copies.new(a0, a0, y_up),
            copies.new(a1, a1, y_down),
            copies.new(a1, a1, y_up),
            copies.new(a0, a0, y_down),
        ]
        for copy in group:
            copy.start()
        return group

    def gather_relay(group, a, to_zh):
        group[0].wait_recv()
        block = a.at[before * 2 + to_zh, low]
        copy = copies.new(block, block, y_up)
        copy.start()
        group.append(copy)
        group[1].wait_recv()
        block = a.at[after * 2 + to_zh, high]
        copy = copies.new(block, block, y_down)
        copy.start()
        group.append(copy)

    def gather_wait(groups, k):
        for group in groups:
            if k == 1:
                group[2].wait_recv()
            elif k == 3:
                group[3].wait_recv()
            else:
                wait_recv(group[4:])

    x_swap = swap_start(in_ref, xa.at[c, zl % 2, d])
    st_core = copies.new(st.at[0], st.at[1], sibling)
    st_core.start()
    g_swap = swap_start(grad_ref, ga.at[c, zl % 2, d])
    st_core.wait_recv()
    mean, square = merge_stats([st[0], st[1]], 128.0)
    st[2] = two_rows(mean, square, 8)
    st_z = [copies.new(st.at[2], st.at[3 + j], peer) for j, peer in enumerate(z_peers)]
    for copy in st_z:
        copy.start()
    x_swap()
    x_z = z_start(xa)
    wait_recv(st_z)
    mean, square = merge_stats([st[2 + j] for j in range(4)], 256.0)
    st[6] = two_rows(mean, square, 8)
    st_x = [copies.new(st.at[6], st.at[7 + j], peer) for j, peer in enumerate(x_peers)]
    for copy in st_x:
        copy.start()
    g_swap()
    g_z = z_start(ga)
    wait_recv(x_z)
    x_x = x_start(xa)
    x_core = to_core(xa, x)
    wait_recv(st_x)
    mean, square = merge_stats([st[6 + j] for j in range(4)], 1024.0)
    inv = 1.0 / jnp.sqrt(square / 4096.0 + 1e-06)
    sa[mine] = two_rows(mean, inv, 8)
    st_far = send_all(sa.at[mine], [far])
    st_y = send_all(sa.at[mine], y_peers)
    x_fars, x_first, x_second = x_forward(xa, x_x)
    wait_recv(g_z)
    g_x = x_start(ga)
    g_core = to_core(ga, x)
    wait_recv(st_far)
    st_y2 = send_all(sa.at[theirs], y_peers)
    g_out = group_plan(pg, lg, rg)
    u_out = group_plan(pu, lu, ru)
    q_out = group_plan(pq, lq, rq)

    def g_step(core, who):
        wait_recv(core)
        products(pg, lambda t: mm_nt(tokens(ga, t), wb[...]), who)
        group_send(g_out, who, (0,))

    def x_step(core, who):
        wait_recv(core)

        def step(i, carry):
            t = 2 * who + i
            columns = jnp.concatenate([sa[t], jnp.zeros((120, TOK), F32)], axis=0).T
            rows = tokens(xa, t).astype(F32)
            xb[t] = ((rows - columns[:, 0:1]) * columns[:, 1:2]).astype(BF)
            return carry

        lax.fori_loop(0, 2, step, 0)
        products(pu, lambda t: mm(xb[t], wu_ref[...]), who)
        group_send(u_out, who, (0,))
        products(pq, lambda t: mm(xb[t], wq[...]), who)
        group_send(q_out, who, (0,))

    wait_recv(st_y + st_y2)
    x_step(x_core, x)
    x_step(x_first, x_before)
    x_step(x_second, x_after)
    wait_recv(x_fars)
    x_step(to_core(xa, x_far), x_far)
    send_own(u_out, 1)
    relay_on(u_out, pu, lu, ru, 0)
    g_fars, g_first, g_second = x_forward(ga, g_x)
    relay_on(q_out, pq, lq, rq, 0)
    send_own(q_out, 1)
    u_far = far_start(u_out, pu, lu, su, zu)
    relay_on(u_out, pu, lu, ru, 1)
    q_far = far_start(q_out, pq, lq, sq, zq)
    g_step(g_core, x)
    g_step(g_first, x_before)
    g_step(g_second, x_after)
    wait_recv(g_fars)
    g_step(to_core(ga, x_far), x_far)
    relay_on(q_out, pq, lq, rq, 1)
    send_own(g_out, 1)
    upper = finish(u_out, u_far, pu, lu, zu)
    erf1 = 1.0 + lax.erf(upper * (1.0 / math.sqrt(2.0)))
    ah[mine] = (0.5 * upper * erf1).astype(BF)
    h_far = gather_far(ah)
    h_y = gather_y(ah, mine)
    slope = 0.5 * erf1 + upper * jnp.exp(-0.5 * upper * upper) * (1.0 / math.sqrt(2.0 * math.pi))
    qkv = finish(q_out, q_far, pq, lq, zq)

    scale = HEAD ** (-0.5)
    q_hat, q_inv = normalize(qkv[:, :128])
    k_hat, k_inv = normalize(qkv[:, 128:256])
    q_n = q_hat.astype(BF)
    k_n = k_hat.astype(BF)
    v_n = qkv[:, 256:].astype(BF)
    expo = jnp.exp(mm_nt(q_n, k_n) * scale)
    prob = expo / jnp.sum(expo, axis=-1, keepdims=True)
    prob_n = prob.astype(BF)
    am[mine] = mm(prob_n, v_n).astype(BF)

    m_far = gather_far(am)
    m_y = gather_y(am, mine)
    relay_on(g_out, pg, lg, rg, 0)
    gather_relay(h_y, ah, zh)
    relay_on(g_out, pg, lg, rg, 1)
    g_far = far_start(g_out, pg, lg, sg, zg)
    h_far.wait_recv()
    h_y2 = gather_y(ah, theirs)
    gather_relay(m_y, am, zh)
    m_far.wait_recv()
    m_y2 = gather_y(am, theirs)
    gather_relay(h_y2, ah, 1 - zh)
    gather_relay(m_y2, am, 1 - zh)
    d_both = finish(g_out, g_far, pg, lg, zg)
    au[mine] = (d_both[:, :384] * slope).astype(BF)
    u_gfar = gather_far(au)
    u_gy = gather_y(au, mine)
    d_mixed = d_both[:, 384:].astype(BF)
    d_prob = mm_nt(d_mixed, v_n)
    d_v = mm_tn(prob_n, d_mixed)
    d_scores = prob * (d_prob - jnp.sum(prob * d_prob, axis=-1, keepdims=True)) * scale
    d_scores = d_scores.astype(BF)
    d_q = norm_back(q_hat, q_inv, mm(d_scores, k_n))
    d_k = norm_back(k_hat, k_inv, mm_tn(d_scores, q_n))
    aq[mine] = jnp.concatenate([d_q, d_k, d_v], axis=1).astype(BF)
    q_gfar = gather_far(aq)
    q_gy = gather_y(aq, mine)
    gather_relay(u_gy, au, zh)

    o_x = [
        copies.new(s1.at[:, pl.ds(2 * ((x + j) % 4), 2)], lx.at[j - 1], x_peers[j - 1])
        for j in (1, 2, 3)
    ]

    def out_product(k):
        if k:
            gather_wait([m_y, m_y2, h_y, h_y2], k)
        g = (y + 4 - k) % 4

        def out_step(i, carry, g=g):
            t = 2 * g + i
            out = mm(jnp.concatenate([ah[t], am[t]], axis=1), wb[...]).astype(BF)
            for cb in range(4):
                lp[cb % 2, cb // 2, t] = out[:, cb * 128 : cb * 128 + 128]
            return carry

        lax.fori_loop(0, 2, out_step, 0)
        copy = copies.new(lp.at[1 - c, :, pl.ds(2 * g, 2)], lc.at[:, pl.ds(2 * g, 2)], sibling)
        copy.start()
        return copy

    def out_core(copy, k):
        copy.wait_recv()
        g = (y + 4 - k) % 4

        def core_step(i, carry):
            t = 2 * g + i
            for b in range(2):
                s1[b, t] = (lp[c, b, t].astype(F32) + lc[b, t].astype(F32)).astype(BF)
            return carry

        lax.fori_loop(0, 2, core_step, 0)
        for j in (1, 2, 3):

            @pl.when((g + 4 - x) % 4 == j)
            def _():
                o_x[j - 1].start()

    c0 = out_product(0)
    c1 = out_product(1)
    c3 = out_product(3)
    out_core(c0, 0)
    c2 = out_product(2)
    out_core(c1, 1)
    gather_relay(q_gy, aq, zh)
    out_core(c3, 3)
    out_core(c2, 2)
    u_gfar.wait_recv()
    u_gy2 = gather_y(au, theirs)
    q_gfar.wait_recv()
    q_gy2 = gather_y(aq, theirs)
    gather_relay(u_gy2, au, 1 - zh)
    acc_b[...] = jnp.zeros_like(acc_b)

    def grad_b(t, carry):
        acc_b[...] += mm_tn(jnp.concatenate([ah[t], am[t]], axis=1), tokens(ga, t))
        return carry

    lax.fori_loop(0, 8, grad_b, 0)

    gather_relay(q_gy2, aq, 1 - zh)
    wait_recv(o_x)
    for b in range(2):
        for i in range(2):
            out = s1[b, 2 * x + i].astype(F32)
            for j in range(3):
                out = out + lx[j, b, i].astype(F32)
            s2[b, i] = out.astype(BF)
    o_z = []
    for j, peer in enumerate(z_peers):
        to = (zl + j + 1) % 4
        copy = copies.new(s2.at[to % 2, to // 2], lz.at[j], peer)
        copy.start()
        o_z.append(copy)

    gd_ref[...] = acc_b[0:384, :].astype(BF)
    go_ref[...] = acc_b[384:512, :].astype(BF)
    acc_x[...] = jnp.zeros_like(acc_x)

    def grad_x(g):
        def step(i, carry):
            t = 2 * g + i
            acc_x[...] += mm_tn(xb[t], jnp.concatenate([aq[t], au[t]], axis=1))
            return carry

        lax.fori_loop(0, 2, step, 0)

    grad_x(y)
    wait_recv(o_z)
    out = s2[zl % 2, zl // 2].astype(F32)
    for j in range(3):
        out = out + lz[j].astype(F32)
    s3[...] = out.astype(BF)
    o_swap = swap_start(s3, fin)
    for k in (1, 3, 2):
        gather_wait([q_gy, q_gy2, u_gy, u_gy2], k)
        grad_x((y + 4 - k) % 4)
    for i in range(3):
        gq_ref[i] = acc_x[:, i * 128 : i * 128 + 128].astype(BF)
    gu_ref[...] = acc_x[:, 384:768].astype(BF)
    o_swap()
    lay_ref[...] = (block_f + fin[...].astype(F32)).astype(BF)

    for copy in copies.all:
        copy.wait_send()

    @pl.when(moves)
    def _():
        for copy in swaps:
            copy.wait_send()


def shards(inputs, qkv_weight, out_weight, up_weight, down_weight, grad_out):
    rows = qkv_weight.shape[0]
    vmem = pl.BlockSpec(memory_space=pltpu.VMEM)

    def buf(*shape, dtype=BF):
        return pltpu.VMEM(shape, dtype)

    layer_out, qkv_grad, out_grad, up_grad, down_grad = pl.pallas_call(
        kernel,
        out_shape=[
            jax.ShapeDtypeStruct(inputs.shape, BF),
            jax.ShapeDtypeStruct((3, rows, 128), BF),
            jax.ShapeDtypeStruct(out_weight.shape, BF),
            jax.ShapeDtypeStruct(up_weight.shape, BF),
            jax.ShapeDtypeStruct(down_weight.shape, BF),
        ],
        in_specs=[vmem] * 6,
        out_specs=[vmem] * 5,
        scratch_shapes=[
            buf(512, 512),
            buf(512, 384),
            buf(8, 8, TOK, dtype=F32),
            buf(8, TOK, 512),
            buf(2, 2, 8, TOK, 128),
            buf(2, 2, 8, TOK, 128),
            buf(10, 8, TOK, dtype=F32),
            buf(8, TOK, 512),
            buf(8, TOK, 384),
            buf(8, TOK, 384),
            buf(2, 2, TOK, 512),
            buf(2, 2, TOK, 384),
            buf(2, 2, TOK, 384),
            buf(2, 2, TOK // 2, 512),
            buf(2, 2, TOK // 2, 384),
            buf(2, 2, TOK // 2, 384),
            buf(TOK, 512),
            buf(TOK, 384),
            buf(TOK, 384),
            buf(TOK, 512),
            buf(TOK, 384),
            buf(TOK, 384),
            buf(8, TOK, 128),
            buf(8, TOK, 384),
            buf(8, TOK, 384),
            buf(8, TOK, 384),
            buf(2, 2, 8, TOK, 128),
            buf(2, 8, TOK, 128),
            buf(2, 8, TOK, 128),
            buf(3, 2, 2, TOK, 128),
            buf(2, 2, TOK, 128),
            buf(3, TOK, 128),
            buf(TOK, 128),
            buf(TOK, 128),
            buf(512, 768, dtype=F32),
            buf(512, 512, dtype=F32),
            pltpu.SemaphoreType.DMA((N_SEMS,)),
            pltpu.SemaphoreType.DMA((N_SEMS,)),
            pltpu.SemaphoreType.DMA((4,)),
        ],
        compiler_params=pltpu.CompilerParams(
            collective_id=0, has_side_effects=True, vmem_limit_bytes=56 * 2**20
        ),
    )(inputs, grad_out, jnp.transpose(qkv_weight, (1, 0, 2)), out_weight, up_weight, down_weight)
    return layer_out, jnp.transpose(qkv_grad, (1, 0, 2)), out_grad, up_grad, down_grad


def solution(mesh):
    placed = (
        P("dp", "mp"),
        P("dp", None, "mp"),
        P("mp", "dp"),
        P("dp", "mp"),
        P("mp", "dp"),
        P("dp", "mp"),
    )
    return jax.shard_map(
        shards,
        mesh=mesh,
        in_specs=placed,
        out_specs=(P("dp", "mp"), P("dp", None, "mp"), P("mp", "dp"), P("dp", "mp"), P("mp", "dp")),
        check_vma=False,
    )
```

```python
import math

import jax
import jax.numpy as jnp
from jax import lax
from jax.experimental import pallas as pl
from jax.experimental.pallas import tpu as pltpu
from jax.sharding import PartitionSpec as P

HEAD = 128
TOK = 256
BF = jnp.bfloat16
F32 = jnp.float32
MESH = pl.DeviceIdType.MESH


def normalize(values):
    centre = values - jnp.mean(values, axis=-1, keepdims=True)
    scale_inv = 1.0 / jnp.sqrt(jnp.mean(centre * centre, axis=-1, keepdims=True) + 1e-06)
    return centre * scale_inv, scale_inv


def norm_back(normed_hat, scale_inv, upstream):
    first = jnp.mean(upstream, axis=-1, keepdims=True)
    second = jnp.mean(upstream * normed_hat, axis=-1, keepdims=True)
    return scale_inv * (upstream - first - normed_hat * second)


def mm(a, b):
    return lax.dot_general(a, b, (((1,), (0,)), ((), ())), preferred_element_type=F32)


def mm_nt(a, b):
    return lax.dot_general(a, b, (((1,), (1,)), ((), ())), preferred_element_type=F32)


def mm_tn(a, b):
    return lax.dot_general(a, b, (((0,), (0,)), ((), ())), preferred_element_type=F32)


def merge_stats(parts, count):
    means = [p[0:1, :] for p in parts]
    mean = sum(means) / len(parts)
    square = sum(p[1:2, :] for p in parts) + count * sum((u - mean) * (u - mean) for u in means)
    return mean, square


def two_rows(first, second, rows):
    place = lax.broadcasted_iota(jnp.int32, (rows, TOK), 0)
    return jnp.where(place == 0, first, jnp.where(place == 1, second, 0.0))


class Copies:
    def __init__(self, send, recv):
        self.send, self.recv, self.used, self.all = send, recv, 0, []

    def take(self, count):
        base = self.used
        self.used += count
        return base

    def make(self, src, dst, device, index):
        return pltpu.make_async_remote_copy(
            src_ref=src,
            dst_ref=dst,
            send_sem=self.send.at[index],
            recv_sem=self.recv.at[index],
            device_id=device,
            device_id_type=MESH,
        )

    def new(self, src, dst, device):
        copy = self.make(src, dst, device, self.take(1))
        self.all.append(copy)
        return copy


N_SEMS = 192


def kernel(
    in_ref, grad_ref, wq_ref, wo_ref, wu_ref, wd_ref,
    lay_ref, gq_ref, go_ref, gu_ref, gd_ref,
    wb, wq, sa, xb, ga, xa, st,
    pg, pq, pu, lg, lq, lu, rg, rq, ru, sg, sq, su, zg, zq, zu,
    am, ah, aq, au,
    lp, lc, s1, lx, s2, lz, s3, fin,
    acc_x, acc_b,
    send, recv, local,
):
    m = lax.axis_index("mp")
    d = lax.axis_index("dp")
    x, zl, c = m // 8, (m // 2) % 4, m % 2
    y, zh = d // 2, d % 2

    def at(x=x, zl=zl, c=c, y=y, zh=zh):
        return {"mp": (x * 4 + zl) * 2 + c, "dp": y * 2 + zh}

    sibling = at(c=1 - c)
    z_peers = [at(zl=(zl + j) % 4) for j in (1, 2, 3)]
    x_peers = [at(x=(x + j) % 4) for j in (1, 2, 3)]
    y_peers = [at(y=(y + k) % 4) for k in (1, 2, 3)]
    y_up, y_down = y_peers[0], y_peers[2]
    far = at(zh=1 - zh)
    swap = at(x=y, zl=2 * zh + zl % 2, y=x, zh=zl // 2)
    stays = jnp.logical_and(x == y, zh == zl // 2)
    moves = jnp.logical_not(stays)

    barrier = pltpu.get_barrier_semaphore()
    near = [sibling, far] + z_peers + x_peers + y_peers
    for device in near:
        pl.semaphore_signal(barrier, inc=1, device_id=device, device_id_type=MESH)

    @pl.when(moves)
    def _():
        pl.semaphore_signal(barrier, inc=1, device_id=swap, device_id_type=MESH)

    block_f = in_ref[...].astype(F32)
    mu = jnp.mean(block_f, axis=-1, keepdims=True)
    centre = block_f - mu
    square = jnp.sum(centre * centre, axis=-1, keepdims=True)
    lane = lax.broadcasted_iota(jnp.int32, (TOK, 128), 1)
    packed = jnp.where(lane == 0, mu, jnp.where(lane == 1, square, 0.0))
    st[0] = packed.T[0:8, :]
    wb[0:384, :] = wd_ref[...]
    wb[384:512, :] = wo_ref[...]
    for i in range(3):
        wq[:, i * 128 : i * 128 + 128] = wq_ref[i]

    @pl.when(moves)
    def _():
        pl.semaphore_wait(barrier, len(near) + 1)

    @pl.when(stays)
    def _():
        pl.semaphore_wait(barrier, len(near))

    copies = Copies(send, recv)
    swaps = []

    def swap_start(src, dst):
        remote = copies.make(src, dst, swap, copies.take(1))
        near_copy = pltpu.make_async_copy(src, dst, local.at[len(swaps)])
        swaps.append(remote)

        @pl.when(moves)
        def _():
            remote.start()

        @pl.when(stays)
        def _():
            near_copy.start()

        def wait():
            @pl.when(moves)
            def _():
                remote.wait_recv()

            @pl.when(stays)
            def _():
                near_copy.wait()

        return wait

    def send_all(block, peers):
        group = [copies.new(block, block, peer) for peer in peers]
        for copy in group:
            copy.start()
        return group

    def z_start(a):
        return send_all(a.at[c, zl % 2, x * 2 + zl // 2], z_peers)

    def half_of(a, who, half):
        return a.at[c, half, pl.ds(2 * who, 2)]

    def to_core(a, who):
        return send_all(a.at[c, :, pl.ds(2 * who, 2)], [sibling])

    def x_start(a):
        up = [copies.new(h, h, x_peers[0]) for h in (half_of(a, x, 0), half_of(a, x, 1))]
        down = [copies.new(h, h, x_peers[2]) for h in (half_of(a, x, 1), half_of(a, x, 0))]
        for pair in zip(up, down):
            for copy in pair:
                copy.start()
        return up, down

    def x_forward(a, group):
        up, down = group
        up[0].wait_recv()
        fars = send_all(half_of(a, x_before, 0), [x_peers[0]])
        down[0].wait_recv()
        fars += send_all(half_of(a, x_after, 1), [x_peers[2]])
        up[1].wait_recv()
        first = to_core(a, x_before)
        down[1].wait_recv()
        return fars, first, to_core(a, x_after)

    def wait_recv(group):
        for copy in group:
            copy.wait_recv()

    def tokens(a, t):
        return jnp.concatenate([a[0, 0, t], a[1, 0, t], a[0, 1, t], a[1, 1, t]], axis=1)

    x_before, x_after, x_far = (x + 3) % 4, (x + 1) % 4, (x + 2) % 4
    mine = d
    theirs = y * 2 + 1 - zh
    before, after = (y + 3) % 4, (y + 1) % 4
    low, high = pl.ds(0, TOK // 2), pl.ds(TOK // 2, TOK // 2)

    def group_plan(p, land, relay):
        out = []
        for own in range(2):
            to_zh = zh if own else 1 - zh
            t = [((y + k) % 4) * 2 + to_zh for k in range(4)]
            out.append([
                copies.new(p.at[t[2], low], relay.at[own, 0], y_up),
                copies.new(p.at[t[2], high], relay.at[own, 1], y_down),
                copies.new(p.at[t[1], high], land.at[own, 0, high], y_up),
                copies.new(p.at[t[3], low], land.at[own, 1, low], y_down),
            ])
        return out

    def group_send(out, who, owns):
        k = (who + 4 - y) % 4

        @pl.when(k == 2)
        def _():
            for own in owns:
                out[own][0].start()
                out[own][1].start()

        @pl.when(k == 1)
        def _():
            for own in owns:
                out[own][2].start()

        @pl.when(k == 3)
        def _():
            for own in owns:
                out[own][3].start()

    def products(p, product, who):
        def step(i, carry):
            t = 2 * who + i
            p[t] = product(t).astype(BF)
            return carry

        lax.fori_loop(0, 2, step, 0)

    def send_own(out, own):
        for copy in out[own][:4]:
            copy.start()

    def products_own(p, product, own):
        to_zh = zh if own else 1 - zh

        def step(i, carry):
            t = 2 * i + to_zh
            p[t] = product(t).astype(BF)
            return carry

        lax.fori_loop(0, 4, step, 0)

    def relay_on(out, p, land, relay, own):
        group = out[own]
        to_zh = zh if own else 1 - zh
        up, down = after * 2 + to_zh, before * 2 + to_zh
        group[0].wait_recv()
        p[up, low] = (p[up, low].astype(F32) + relay[own, 0].astype(F32)).astype(BF)
        copy = copies.new(p.at[up, low], land.at[own, 0, low], y_up)
        copy.start()
        group.append(copy)
        group[1].wait_recv()
        p[down, high] = (p[down, high].astype(F32) + relay[own, 1].astype(F32)).astype(BF)
        copy = copies.new(p.at[down, high], land.at[own, 1, high], y_down)
        copy.start()
        group.append(copy)

    def total(p, land, own, t):
        return p[t].astype(F32) + land[own, 0].astype(F32) + land[own, 1].astype(F32)

    def far_start(out, p, land, s, z):
        wait_recv(out[0][2:])
        s[...] = total(p, land, 0, theirs).astype(BF)
        copy = copies.new(s, z, far)
        copy.start()
        return copy

    def finish(out, copy, p, land, z):
        wait_recv(out[1][2:])
        copy.wait_recv()
        return total(p, land, 1, mine) + z[...].astype(F32)

    def gather_far(a):
        copy = copies.new(a.at[mine], a.at[mine], far)
        copy.start()
        return copy

    def gather_y(a, t):
        a0, a1 = a.at[t, low], a.at[t, high]
        group = [
            copies.new(a0, a0, y_up),
            copies.new(a1, a1, y_down),
            copies.new(a1, a1, y_up),
            copies.new(a0, a0, y_down),
        ]
        for copy in group:
            copy.start()
        return group

    def gather_relay(group, a, to_zh):
        group[0].wait_recv()
        block = a.at[before * 2 + to_zh, low]
        copy = copies.new(block, block, y_up)
        copy.start()
        group.append(copy)
        group[1].wait_recv()
        block = a.at[after * 2 + to_zh, high]
        copy = copies.new(block, block, y_down)
        copy.start()
        group.append(copy)

    def gather_wait(groups, k):
        for group in groups:
            if k == 1:
                group[2].wait_recv()
            elif k == 3:
                group[3].wait_recv()
            else:
                wait_recv(group[4:])

    x_swap = swap_start(in_ref, xa.at[c, zl % 2, d])
    st_core = copies.new(st.at[0], st.at[1], sibling)
    st_core.start()
    st_core.wait_recv()
    mean, square = merge_stats([st[0], st[1]], 128.0)
    st[2] = two_rows(mean, square, 8)
    st_z = [copies.new(st.at[2], st.at[3 + j], peer) for j, peer in enumerate(z_peers)]
    for copy in st_z:
        copy.start()
    x_swap()
    x_z = z_start(xa)
    g_swap = swap_start(grad_ref, ga.at[c, zl % 2, d])
    wait_recv(st_z)
    mean, square = merge_stats([st[2 + j] for j in range(4)], 256.0)
    st[6] = two_rows(mean, square, 8)
    st_x = [copies.new(st.at[6], st.at[7 + j], peer) for j, peer in enumerate(x_peers)]
    for copy in st_x:
        copy.start()
    wait_recv(x_z)
    x_x = x_start(xa)
    x_core = to_core(xa, x)
    wait_recv(st_x)
    mean, square = merge_stats([st[6 + j] for j in range(4)], 1024.0)
    inv = 1.0 / jnp.sqrt(square / 4096.0 + 1e-06)
    sa[mine] = two_rows(mean, inv, 8)
    st_far = send_all(sa.at[mine], [far])
    st_y = send_all(sa.at[mine], y_peers)
    x_fars, x_first, x_second = x_forward(xa, x_x)
    wait_recv(st_far)
    st_y2 = send_all(sa.at[theirs], y_peers)
    g_swap()
    g_z = z_start(ga)
    g_out = group_plan(pg, lg, rg)
    u_out = group_plan(pu, lu, ru)
    q_out = group_plan(pq, lq, rq)

    def g_step(core, who):
        wait_recv(core)
        products(pg, lambda t: mm_nt(tokens(ga, t), wb[...]), who)
        group_send(g_out, who, (0,))

    def x_step(core, who):
        wait_recv(core)

        def step(i, carry):
            t = 2 * who + i
            columns = jnp.concatenate([sa[t], jnp.zeros((120, TOK), F32)], axis=0).T
            rows = tokens(xa, t).astype(F32)
            xb[t] = ((rows - columns[:, 0:1]) * columns[:, 1:2]).astype(BF)
            return carry

        lax.fori_loop(0, 2, step, 0)
        products(pu, lambda t: mm(xb[t], wu_ref[...]), who)
        group_send(u_out, who, (0,))
        products(pq, lambda t: mm(xb[t], wq[...]), who)
        group_send(q_out, who, (0,))

    wait_recv(st_y + st_y2)
    x_step(x_core, x)
    x_step(x_first, x_before)
    x_step(x_second, x_after)
    wait_recv(x_fars)
    x_last = to_core(xa, x_far)
    wait_recv(g_z)
    g_x = x_start(ga)
    g_core = to_core(ga, x)
    x_step(x_last, x_far)
    send_own(u_out, 1)
    relay_on(u_out, pu, lu, ru, 0)
    g_fars, g_first, g_second = x_forward(ga, g_x)
    relay_on(q_out, pq, lq, rq, 0)
    send_own(q_out, 1)
    u_far = far_start(u_out, pu, lu, su, zu)
    relay_on(u_out, pu, lu, ru, 1)
    q_far = far_start(q_out, pq, lq, sq, zq)
    g_step(g_core, x)
    g_step(g_first, x_before)
    g_step(g_second, x_after)
    wait_recv(g_fars)
    g_step(to_core(ga, x_far), x_far)
    relay_on(q_out, pq, lq, rq, 1)
    send_own(g_out, 1)
    upper = finish(u_out, u_far, pu, lu, zu)
    erf1 = 1.0 + lax.erf(upper * (1.0 / math.sqrt(2.0)))
    ah[mine] = (0.5 * upper * erf1).astype(BF)
    h_far = gather_far(ah)
    h_y = gather_y(ah, mine)
    slope = 0.5 * erf1 + upper * jnp.exp(-0.5 * upper * upper) * (1.0 / math.sqrt(2.0 * math.pi))
    qkv = finish(q_out, q_far, pq, lq, zq)

    scale = HEAD ** (-0.5)
    q_hat, q_inv = normalize(qkv[:, :128])
    k_hat, k_inv = normalize(qkv[:, 128:256])
    q_n = q_hat.astype(BF)
    k_n = k_hat.astype(BF)
    v_n = qkv[:, 256:].astype(BF)
    expo = jnp.exp(mm_nt(q_n, k_n) * scale)
    prob = expo / jnp.sum(expo, axis=-1, keepdims=True)
    prob_n = prob.astype(BF)
    am[mine] = mm(prob_n, v_n).astype(BF)

    m_far = gather_far(am)
    m_y = gather_y(am, mine)
    relay_on(g_out, pg, lg, rg, 0)
    gather_relay(h_y, ah, zh)
    relay_on(g_out, pg, lg, rg, 1)
    g_far = far_start(g_out, pg, lg, sg, zg)
    h_far.wait_recv()
    h_y2 = gather_y(ah, theirs)
    gather_relay(m_y, am, zh)
    m_far.wait_recv()
    m_y2 = gather_y(am, theirs)
    gather_relay(h_y2, ah, 1 - zh)
    gather_relay(m_y2, am, 1 - zh)
    d_both = finish(g_out, g_far, pg, lg, zg)
    au[mine] = (d_both[:, :384] * slope).astype(BF)
    u_gfar = gather_far(au)
    u_gy = gather_y(au, mine)
    d_mixed = d_both[:, 384:].astype(BF)
    d_prob = mm_nt(d_mixed, v_n)
    d_v = mm_tn(prob_n, d_mixed)
    d_scores = prob * (d_prob - jnp.sum(prob * d_prob, axis=-1, keepdims=True)) * scale
    d_scores = d_scores.astype(BF)
    d_q = norm_back(q_hat, q_inv, mm(d_scores, k_n))
    d_k = norm_back(k_hat, k_inv, mm_tn(d_scores, q_n))
    aq[mine] = jnp.concatenate([d_q, d_k, d_v], axis=1).astype(BF)
    q_gfar = gather_far(aq)
    q_gy = gather_y(aq, mine)
    o_x = [
        copies.new(s1.at[:, pl.ds(2 * ((x + j) % 4), 2)], lx.at[j - 1], x_peers[j - 1])
        for j in (1, 2, 3)
    ]

    def out_product(k):
        if k:
            gather_wait([m_y, m_y2, h_y, h_y2], k)
        g = (y + 4 - k) % 4

        def out_step(i, carry, g=g):
            t = 2 * g + i
            out = mm(jnp.concatenate([ah[t], am[t]], axis=1), wb[...]).astype(BF)
            for cb in range(4):
                lp[cb % 2, cb // 2, t] = out[:, cb * 128 : cb * 128 + 128]
            return carry

        lax.fori_loop(0, 2, out_step, 0)
        copy = copies.new(lp.at[1 - c, :, pl.ds(2 * g, 2)], lc.at[:, pl.ds(2 * g, 2)], sibling)
        copy.start()
        return copy

    def out_core(copy, k):
        copy.wait_recv()
        g = (y + 4 - k) % 4

        def core_step(i, carry):
            t = 2 * g + i
            for b in range(2):
                s1[b, t] = (lp[c, b, t].astype(F32) + lc[b, t].astype(F32)).astype(BF)
            return carry

        lax.fori_loop(0, 2, core_step, 0)
        for j in (1, 2, 3):

            @pl.when((g + 4 - x) % 4 == j)
            def _():
                o_x[j - 1].start()

    c0 = out_product(0)
    c1 = out_product(1)
    c3 = out_product(3)
    out_core(c0, 0)
    gather_relay(u_gy, au, zh)
    c2 = out_product(2)
    out_core(c1, 1)
    out_core(c3, 3)
    gather_relay(q_gy, aq, zh)
    out_core(c2, 2)
    u_gfar.wait_recv()
    u_gy2 = gather_y(au, theirs)
    q_gfar.wait_recv()
    q_gy2 = gather_y(aq, theirs)
    gather_relay(u_gy2, au, 1 - zh)
    acc_b[...] = jnp.zeros_like(acc_b)

    def grad_b(t, carry):
        acc_b[...] += mm_tn(jnp.concatenate([ah[t], am[t]], axis=1), tokens(ga, t))
        return carry

    lax.fori_loop(0, 8, grad_b, 0)

    gather_relay(q_gy2, aq, 1 - zh)
    wait_recv(o_x)
    for b in range(2):
        for i in range(2):
            out = s1[b, 2 * x + i].astype(F32)
            for j in range(3):
                out = out + lx[j, b, i].astype(F32)
            s2[b, i] = out.astype(BF)
    o_z = []
    for j, peer in enumerate(z_peers):
        to = (zl + j + 1) % 4
        copy = copies.new(s2.at[to % 2, to // 2], lz.at[j], peer)
        copy.start()
        o_z.append(copy)

    gd_ref[...] = acc_b[0:384, :].astype(BF)
    go_ref[...] = acc_b[384:512, :].astype(BF)
    acc_x[...] = jnp.zeros_like(acc_x)

    def grad_x(g):
        def step(i, carry):
            t = 2 * g + i
            acc_x[...] += mm_tn(xb[t], jnp.concatenate([aq[t], au[t]], axis=1))
            return carry

        lax.fori_loop(0, 2, step, 0)

    grad_x(y)
    wait_recv(o_z)
    out = s2[zl % 2, zl // 2].astype(F32)
    for j in range(3):
        out = out + lz[j].astype(F32)
    s3[...] = out.astype(BF)
    o_swap = swap_start(s3, fin)
    for k in (1, 3, 2):
        gather_wait([q_gy, q_gy2, u_gy, u_gy2], k)
        grad_x((y + 4 - k) % 4)
    for i in range(3):
        gq_ref[i] = acc_x[:, i * 128 : i * 128 + 128].astype(BF)
    gu_ref[...] = acc_x[:, 384:768].astype(BF)
    o_swap()
    lay_ref[...] = (block_f + fin[...].astype(F32)).astype(BF)

    for copy in copies.all:
        copy.wait_send()

    @pl.when(moves)
    def _():
        for copy in swaps:
            copy.wait_send()


def shards(inputs, qkv_weight, out_weight, up_weight, down_weight, grad_out):
    rows = qkv_weight.shape[0]
    vmem = pl.BlockSpec(memory_space=pltpu.VMEM)

    def buf(*shape, dtype=BF):
        return pltpu.VMEM(shape, dtype)

    layer_out, qkv_grad, out_grad, up_grad, down_grad = pl.pallas_call(
        kernel,
        out_shape=[
            jax.ShapeDtypeStruct(inputs.shape, BF),
            jax.ShapeDtypeStruct((3, rows, 128), BF),
            jax.ShapeDtypeStruct(out_weight.shape, BF),
            jax.ShapeDtypeStruct(up_weight.shape, BF),
            jax.ShapeDtypeStruct(down_weight.shape, BF),
        ],
        in_specs=[vmem] * 6,
        out_specs=[vmem] * 5,
        scratch_shapes=[
            buf(512, 512),
            buf(512, 384),
            buf(8, 8, TOK, dtype=F32),
            buf(8, TOK, 512),
            buf(2, 2, 8, TOK, 128),
            buf(2, 2, 8, TOK, 128),
            buf(10, 8, TOK, dtype=F32),
            buf(8, TOK, 512),
            buf(8, TOK, 384),
            buf(8, TOK, 384),
            buf(2, 2, TOK, 512),
            buf(2, 2, TOK, 384),
            buf(2, 2, TOK, 384),
            buf(2, 2, TOK // 2, 512),
            buf(2, 2, TOK // 2, 384),
            buf(2, 2, TOK // 2, 384),
            buf(TOK, 512),
            buf(TOK, 384),
            buf(TOK, 384),
            buf(TOK, 512),
            buf(TOK, 384),
            buf(TOK, 384),
            buf(8, TOK, 128),
            buf(8, TOK, 384),
            buf(8, TOK, 384),
            buf(8, TOK, 384),
            buf(2, 2, 8, TOK, 128),
            buf(2, 8, TOK, 128),
            buf(2, 8, TOK, 128),
            buf(3, 2, 2, TOK, 128),
            buf(2, 2, TOK, 128),
            buf(3, TOK, 128),
            buf(TOK, 128),
            buf(TOK, 128),
            buf(512, 768, dtype=F32),
            buf(512, 512, dtype=F32),
            pltpu.SemaphoreType.DMA((N_SEMS,)),
            pltpu.SemaphoreType.DMA((N_SEMS,)),
            pltpu.SemaphoreType.DMA((4,)),
        ],
        compiler_params=pltpu.CompilerParams(
            collective_id=0, has_side_effects=True, vmem_limit_bytes=56 * 2**20
        ),
    )(inputs, grad_out, jnp.transpose(qkv_weight, (1, 0, 2)), out_weight, up_weight, down_weight)
    return layer_out, jnp.transpose(qkv_grad, (1, 0, 2)), out_grad, up_grad, down_grad


def solution(mesh):
    placed = (
        P("dp", "mp"),
        P("dp", None, "mp"),
        P("mp", "dp"),
        P("dp", "mp"),
        P("mp", "dp"),
        P("dp", "mp"),
    )
    return jax.shard_map(
        shards,
        mesh=mesh,
        in_specs=placed,
        out_specs=(P("dp", "mp"), P("dp", None, "mp"), P("mp", "dp"), P("dp", "mp"), P("mp", "dp")),
        check_vma=False,
    )
```

```python
import math

import jax
import jax.numpy as jnp
from jax import lax
from jax.experimental import pallas as pl
from jax.experimental.pallas import tpu as pltpu
from jax.sharding import PartitionSpec as P

HEAD = 128
TOK = 256
BF = jnp.bfloat16
F32 = jnp.float32
MESH = pl.DeviceIdType.MESH


def normalize(values):
    centre = values - jnp.mean(values, axis=-1, keepdims=True)
    scale_inv = 1.0 / jnp.sqrt(jnp.mean(centre * centre, axis=-1, keepdims=True) + 1e-06)
    return centre * scale_inv, scale_inv


def norm_back(normed_hat, scale_inv, upstream):
    first = jnp.mean(upstream, axis=-1, keepdims=True)
    second = jnp.mean(upstream * normed_hat, axis=-1, keepdims=True)
    return scale_inv * (upstream - first - normed_hat * second)


def mm(a, b):
    return lax.dot_general(a, b, (((1,), (0,)), ((), ())), preferred_element_type=F32)


def mm_nt(a, b):
    return lax.dot_general(a, b, (((1,), (1,)), ((), ())), preferred_element_type=F32)


def mm_tn(a, b):
    return lax.dot_general(a, b, (((0,), (0,)), ((), ())), preferred_element_type=F32)


def merge_stats(parts, count):
    means = [p[0:1, :] for p in parts]
    mean = sum(means) / len(parts)
    square = sum(p[1:2, :] for p in parts) + count * sum((u - mean) * (u - mean) for u in means)
    return mean, square


def two_rows(first, second, rows):
    place = lax.broadcasted_iota(jnp.int32, (rows, TOK), 0)
    return jnp.where(place == 0, first, jnp.where(place == 1, second, 0.0))


class Copies:
    def __init__(self, send, recv):
        self.send, self.recv, self.used, self.all = send, recv, 0, []

    def take(self, count):
        base = self.used
        self.used += count
        return base

    def make(self, src, dst, device, index):
        return pltpu.make_async_remote_copy(
            src_ref=src,
            dst_ref=dst,
            send_sem=self.send.at[index],
            recv_sem=self.recv.at[index],
            device_id=device,
            device_id_type=MESH,
        )

    def new(self, src, dst, device):
        copy = self.make(src, dst, device, self.take(1))
        self.all.append(copy)
        return copy


N_SEMS = 192


def kernel(
    in_ref, grad_ref, wq_ref, wo_ref, wu_ref, wd_ref,
    lay_ref, gq_ref, go_ref, gu_ref, gd_ref,
    wb, wq, sa, xb, ga, xa, st,
    pg, pq, pu, lg, lq, lu, rg, rq, ru, sg, sq, su, zg, zq, zu,
    am, ah, aq, au,
    lp, lc, s1, lx, s2, lz, s3, fin,
    acc_x, acc_b,
    send, recv, local,
):
    m = lax.axis_index("mp")
    d = lax.axis_index("dp")
    x, zl, c = m // 8, (m // 2) % 4, m % 2
    y, zh = d // 2, d % 2

    def at(x=x, zl=zl, c=c, y=y, zh=zh):
        return {"mp": (x * 4 + zl) * 2 + c, "dp": y * 2 + zh}

    sibling = at(c=1 - c)
    z_peers = [at(zl=(zl + j) % 4) for j in (1, 2, 3)]
    x_peers = [at(x=(x + j) % 4) for j in (1, 2, 3)]
    y_peers = [at(y=(y + k) % 4) for k in (1, 2, 3)]
    y_up, y_down = y_peers[0], y_peers[2]
    far = at(zh=1 - zh)
    swap = at(x=y, zl=2 * zh + zl % 2, y=x, zh=zl // 2)
    stays = jnp.logical_and(x == y, zh == zl // 2)
    moves = jnp.logical_not(stays)

    barrier = pltpu.get_barrier_semaphore()
    near = [sibling, far] + z_peers + x_peers + y_peers
    for device in near:
        pl.semaphore_signal(barrier, inc=1, device_id=device, device_id_type=MESH)

    @pl.when(moves)
    def _():
        pl.semaphore_signal(barrier, inc=1, device_id=swap, device_id_type=MESH)

    block_f = in_ref[...].astype(F32)
    mu = jnp.mean(block_f, axis=-1, keepdims=True)
    centre = block_f - mu
    square = jnp.sum(centre * centre, axis=-1, keepdims=True)
    lane = lax.broadcasted_iota(jnp.int32, (TOK, 128), 1)
    packed = jnp.where(lane == 0, mu, jnp.where(lane == 1, square, 0.0))
    st[0] = packed.T[0:8, :]
    wb[0:384, :] = wd_ref[...]
    wb[384:512, :] = wo_ref[...]
    for i in range(3):
        wq[:, i * 128 : i * 128 + 128] = wq_ref[i]

    @pl.when(moves)
    def _():
        pl.semaphore_wait(barrier, len(near) + 1)

    @pl.when(stays)
    def _():
        pl.semaphore_wait(barrier, len(near))

    copies = Copies(send, recv)
    swaps = []

    def swap_start(src, dst):
        remote = copies.make(src, dst, swap, copies.take(1))
        near_copy = pltpu.make_async_copy(src, dst, local.at[len(swaps)])
        swaps.append(remote)

        @pl.when(moves)
        def _():
            remote.start()

        @pl.when(stays)
        def _():
            near_copy.start()

        def wait():
            @pl.when(moves)
            def _():
                remote.wait_recv()

            @pl.when(stays)
            def _():
                near_copy.wait()

        return wait

    def send_all(block, peers):
        group = [copies.new(block, block, peer) for peer in peers]
        for copy in group:
            copy.start()
        return group

    def z_start(a):
        return send_all(a.at[c, zl % 2, x * 2 + zl // 2], z_peers)

    def half_of(a, who, half):
        return a.at[c, half, pl.ds(2 * who, 2)]

    def to_core(a, who):
        return send_all(a.at[c, :, pl.ds(2 * who, 2)], [sibling])

    def x_start(a):
        up = [copies.new(h, h, x_peers[0]) for h in (half_of(a, x, 0), half_of(a, x, 1))]
        down = [copies.new(h, h, x_peers[2]) for h in (half_of(a, x, 1), half_of(a, x, 0))]
        for pair in zip(up, down):
            for copy in pair:
                copy.start()
        return up, down

    def x_forward(a, group):
        up, down = group
        up[0].wait_recv()
        fars = send_all(half_of(a, x_before, 0), [x_peers[0]])
        down[0].wait_recv()
        fars += send_all(half_of(a, x_after, 1), [x_peers[2]])
        up[1].wait_recv()
        first = to_core(a, x_before)
        down[1].wait_recv()
        return fars, first, to_core(a, x_after)

    def wait_recv(group):
        for copy in group:
            copy.wait_recv()

    def tokens(a, t):
        return jnp.concatenate([a[0, 0, t], a[1, 0, t], a[0, 1, t], a[1, 1, t]], axis=1)

    x_before, x_after, x_far = (x + 3) % 4, (x + 1) % 4, (x + 2) % 4
    mine = d
    theirs = y * 2 + 1 - zh
    before, after = (y + 3) % 4, (y + 1) % 4
    low, high = pl.ds(0, TOK // 2), pl.ds(TOK // 2, TOK // 2)

    def group_plan(p, land, relay):
        out = []
        for own in range(2):
            to_zh = zh if own else 1 - zh
            t = [((y + k) % 4) * 2 + to_zh for k in range(4)]
            out.append([
                copies.new(p.at[t[2], low], relay.at[own, 0], y_up),
                copies.new(p.at[t[2], high], relay.at[own, 1], y_down),
                copies.new(p.at[t[1], high], land.at[own, 0, high], y_up),
                copies.new(p.at[t[3], low], land.at[own, 1, low], y_down),
            ])
        return out

    def group_send(out, who, owns):
        k = (who + 4 - y) % 4

        @pl.when(k == 2)
        def _():
            for own in owns:
                out[own][0].start()
                out[own][1].start()

        @pl.when(k == 1)
        def _():
            for own in owns:
                out[own][2].start()

        @pl.when(k == 3)
        def _():
            for own in owns:
                out[own][3].start()

    def products(p, product, who):
        def step(i, carry):
            t = 2 * who + i
            p[t] = product(t).astype(BF)
            return carry

        lax.fori_loop(0, 2, step, 0)

    def send_own(out, own):
        for copy in out[own][:4]:
            copy.start()

    def products_own(p, product, own):
        to_zh = zh if own else 1 - zh

        def step(i, carry):
            t = 2 * i + to_zh
            p[t] = product(t).astype(BF)
            return carry

        lax.fori_loop(0, 4, step, 0)

    def relay_on(out, p, land, relay, own):
        group = out[own]
        to_zh = zh if own else 1 - zh
        up, down = after * 2 + to_zh, before * 2 + to_zh
        group[0].wait_recv()
        p[up, low] = (p[up, low].astype(F32) + relay[own, 0].astype(F32)).astype(BF)
        copy = copies.new(p.at[up, low], land.at[own, 0, low], y_up)
        copy.start()
        group.append(copy)
        group[1].wait_recv()
        p[down, high] = (p[down, high].astype(F32) + relay[own, 1].astype(F32)).astype(BF)
        copy = copies.new(p.at[down, high], land.at[own, 1, high], y_down)
        copy.start()
        group.append(copy)

    def total(p, land, own, t):
        return p[t].astype(F32) + land[own, 0].astype(F32) + land[own, 1].astype(F32)

    def far_start(out, p, land, s, z):
        wait_recv(out[0][2:])
        s[...] = total(p, land, 0, theirs).astype(BF)
        copy = copies.new(s, z, far)
        copy.start()
        return copy

    def finish(out, copy, p, land, z):
        wait_recv(out[1][2:])
        copy.wait_recv()
        return total(p, land, 1, mine) + z[...].astype(F32)

    def gather_far(a):
        copy = copies.new(a.at[mine], a.at[mine], far)
        copy.start()
        return copy

    def gather_y(a, t):
        a0, a1 = a.at[t, low], a.at[t, high]
        group = [
            copies.new(a0, a0, y_up),
            copies.new(a1, a1, y_down),
            copies.new(a1, a1, y_up),
            copies.new(a0, a0, y_down),
        ]
        for copy in group:
            copy.start()
        return group

    def gather_relay(group, a, to_zh):
        group[0].wait_recv()
        block = a.at[before * 2 + to_zh, low]
        copy = copies.new(block, block, y_up)
        copy.start()
        group.append(copy)
        group[1].wait_recv()
        block = a.at[after * 2 + to_zh, high]
        copy = copies.new(block, block, y_down)
        copy.start()
        group.append(copy)

    def gather_wait(groups, k):
        for group in groups:
            if k == 1:
                group[2].wait_recv()
            elif k == 3:
                group[3].wait_recv()
            else:
                wait_recv(group[4:])

    x_swap = swap_start(in_ref, xa.at[c, zl % 2, d])
    st_core = copies.new(st.at[0], st.at[1], sibling)
    st_core.start()
    st_core.wait_recv()
    mean, square = merge_stats([st[0], st[1]], 128.0)
    st[2] = two_rows(mean, square, 8)
    st_z = [copies.new(st.at[2], st.at[3 + j], peer) for j, peer in enumerate(z_peers)]
    for copy in st_z:
        copy.start()
    x_swap()
    x_z = z_start(xa)
    g_swap = swap_start(grad_ref, ga.at[c, zl % 2, d])
    wait_recv(st_z)
    mean, square = merge_stats([st[2 + j] for j in range(4)], 256.0)
    st[6] = two_rows(mean, square, 8)
    st_x = [copies.new(st.at[6], st.at[7 + j], peer) for j, peer in enumerate(x_peers)]
    for copy in st_x:
        copy.start()
    wait_recv(x_z)
    x_x = x_start(xa)
    x_core = to_core(xa, x)
    wait_recv(st_x)
    mean, square = merge_stats([st[6 + j] for j in range(4)], 1024.0)
    inv = 1.0 / jnp.sqrt(square / 4096.0 + 1e-06)
    sa[mine] = two_rows(mean, inv, 8)
    st_far = send_all(sa.at[mine], [far])
    st_y = send_all(sa.at[mine], y_peers)
    x_fars, x_first, x_second = x_forward(xa, x_x)
    wait_recv(st_far)
    st_y2 = send_all(sa.at[theirs], y_peers)
    g_swap()
    g_z = z_start(ga)
    g_out = group_plan(pg, lg, rg)
    u_out = group_plan(pu, lu, ru)
    q_out = group_plan(pq, lq, rq)

    def g_step(core, who):
        wait_recv(core)
        products(pg, lambda t: mm_nt(tokens(ga, t), wb[...]), who)
        group_send(g_out, who, (0,))

    def x_step(core, who):
        wait_recv(core)

        def step(i, carry):
            t = 2 * who + i
            columns = jnp.concatenate([sa[t], jnp.zeros((120, TOK), F32)], axis=0).T
            rows = tokens(xa, t).astype(F32)
            xb[t] = ((rows - columns[:, 0:1]) * columns[:, 1:2]).astype(BF)
            return carry

        lax.fori_loop(0, 2, step, 0)
        products(pu, lambda t: mm(xb[t], wu_ref[...]), who)
        group_send(u_out, who, (0,))
        products(pq, lambda t: mm(xb[t], wq[...]), who)
        group_send(q_out, who, (0,))

    wait_recv(st_y + st_y2)
    x_step(x_core, x)
    x_step(x_first, x_before)
    x_step(x_second, x_after)
    wait_recv(x_fars)
    x_last = to_core(xa, x_far)
    wait_recv(g_z)
    g_x = x_start(ga)
    g_core = to_core(ga, x)
    x_step(x_last, x_far)
    send_own(u_out, 1)
    relay_on(u_out, pu, lu, ru, 0)
    g_fars, g_first, g_second = x_forward(ga, g_x)
    relay_on(q_out, pq, lq, rq, 0)
    send_own(q_out, 1)
    u_far = far_start(u_out, pu, lu, su, zu)
    relay_on(u_out, pu, lu, ru, 1)
    q_far = far_start(q_out, pq, lq, sq, zq)
    g_step(g_core, x)
    g_step(g_first, x_before)
    g_step(g_second, x_after)
    wait_recv(g_fars)
    g_step(to_core(ga, x_far), x_far)
    relay_on(q_out, pq, lq, rq, 1)
    send_own(g_out, 1)
    upper = finish(u_out, u_far, pu, lu, zu)
    erf1 = 1.0 + lax.erf(upper * (1.0 / math.sqrt(2.0)))
    ah[mine] = (0.5 * upper * erf1).astype(BF)
    h_far = gather_far(ah)
    h_y = gather_y(ah, mine)
    slope = 0.5 * erf1 + upper * jnp.exp(-0.5 * upper * upper) * (1.0 / math.sqrt(2.0 * math.pi))
    qkv = finish(q_out, q_far, pq, lq, zq)

    scale = HEAD ** (-0.5)
    q_hat, q_inv = normalize(qkv[:, :128])
    k_hat, k_inv = normalize(qkv[:, 128:256])
    q_n = q_hat.astype(BF)
    k_n = k_hat.astype(BF)
    v_n = qkv[:, 256:].astype(BF)
    expo = jnp.exp(mm_nt(q_n, k_n) * scale)
    prob = expo / jnp.sum(expo, axis=-1, keepdims=True)
    prob_n = prob.astype(BF)
    am[mine] = mm(prob_n, v_n).astype(BF)

    m_far = gather_far(am)
    m_y = gather_y(am, mine)
    relay_on(g_out, pg, lg, rg, 0)
    gather_relay(h_y, ah, zh)
    relay_on(g_out, pg, lg, rg, 1)
    g_far = far_start(g_out, pg, lg, sg, zg)
    h_far.wait_recv()
    h_y2 = gather_y(ah, theirs)
    gather_relay(m_y, am, zh)
    m_far.wait_recv()
    m_y2 = gather_y(am, theirs)
    gather_relay(h_y2, ah, 1 - zh)
    gather_relay(m_y2, am, 1 - zh)
    d_both = finish(g_out, g_far, pg, lg, zg)
    au[mine] = (d_both[:, :384] * slope).astype(BF)
    u_gfar = gather_far(au)
    u_gy = gather_y(au, mine)
    d_mixed = d_both[:, 384:].astype(BF)
    d_prob = mm_nt(d_mixed, v_n)
    d_v = mm_tn(prob_n, d_mixed)
    d_scores = prob * (d_prob - jnp.sum(prob * d_prob, axis=-1, keepdims=True)) * scale
    d_scores = d_scores.astype(BF)
    d_q = norm_back(q_hat, q_inv, mm(d_scores, k_n))
    d_k = norm_back(k_hat, k_inv, mm_tn(d_scores, q_n))
    aq[mine] = jnp.concatenate([d_q, d_k, d_v], axis=1).astype(BF)
    q_gfar = gather_far(aq)
    q_gy = gather_y(aq, mine)
    o_x = [
        copies.new(s1.at[:, pl.ds(2 * ((x + j) % 4), 2)], lx.at[j - 1], x_peers[j - 1])
        for j in (1, 2, 3)
    ]

    def out_product(k):
        if k:
            gather_wait([m_y, m_y2, h_y, h_y2], k)
        g = (y + 4 - k) % 4

        def out_step(i, carry, g=g):
            t = 2 * g + i
            out = mm(jnp.concatenate([ah[t], am[t]], axis=1), wb[...]).astype(BF)
            for cb in range(4):
                lp[cb % 2, cb // 2, t] = out[:, cb * 128 : cb * 128 + 128]
            return carry

        lax.fori_loop(0, 2, out_step, 0)
        copy = copies.new(lp.at[1 - c, :, pl.ds(2 * g, 2)], lc.at[:, pl.ds(2 * g, 2)], sibling)
        copy.start()
        return copy

    def out_core(copy, k):
        copy.wait_recv()
        g = (y + 4 - k) % 4

        def core_step(i, carry):
            t = 2 * g + i
            for b in range(2):
                s1[b, t] = (lp[c, b, t].astype(F32) + lc[b, t].astype(F32)).astype(BF)
            return carry

        lax.fori_loop(0, 2, core_step, 0)
        for j in (1, 2, 3):

            @pl.when((g + 4 - x) % 4 == j)
            def _():
                o_x[j - 1].start()

    c0 = out_product(0)
    c1 = out_product(1)
    c3 = out_product(3)
    out_core(c0, 0)
    gather_relay(u_gy, au, zh)
    c2 = out_product(2)
    out_core(c1, 1)
    out_core(c3, 3)
    gather_relay(q_gy, aq, zh)
    u_gfar.wait_recv()
    u_gy2 = gather_y(au, theirs)
    out_core(c2, 2)
    q_gfar.wait_recv()
    q_gy2 = gather_y(aq, theirs)
    gather_relay(u_gy2, au, 1 - zh)
    acc_b[...] = jnp.zeros_like(acc_b)

    def grad_b(t, carry):
        acc_b[...] += mm_tn(jnp.concatenate([ah[t], am[t]], axis=1), tokens(ga, t))
        return carry

    lax.fori_loop(0, 8, grad_b, 0)

    gather_relay(q_gy2, aq, 1 - zh)
    wait_recv(o_x)
    for b in range(2):
        for i in range(2):
            out = s1[b, 2 * x + i].astype(F32)
            for j in range(3):
                out = out + lx[j, b, i].astype(F32)
            s2[b, i] = out.astype(BF)
    o_z = []
    for j, peer in enumerate(z_peers):
        to = (zl + j + 1) % 4
        copy = copies.new(s2.at[to % 2, to // 2], lz.at[j], peer)
        copy.start()
        o_z.append(copy)

    gd_ref[...] = acc_b[0:384, :].astype(BF)
    go_ref[...] = acc_b[384:512, :].astype(BF)
    acc_x[...] = jnp.zeros_like(acc_x)

    def grad_x(g):
        def step(i, carry):
            t = 2 * g + i
            acc_x[...] += mm_tn(xb[t], jnp.concatenate([aq[t], au[t]], axis=1))
            return carry

        lax.fori_loop(0, 2, step, 0)

    grad_x(y)
    wait_recv(o_z)
    out = s2[zl % 2, zl // 2].astype(F32)
    for j in range(3):
        out = out + lz[j].astype(F32)
    s3[...] = out.astype(BF)
    o_swap = swap_start(s3, fin)
    for k in (1, 3, 2):
        gather_wait([q_gy, q_gy2, u_gy, u_gy2], k)
        grad_x((y + 4 - k) % 4)
    for i in range(3):
        gq_ref[i] = acc_x[:, i * 128 : i * 128 + 128].astype(BF)
    gu_ref[...] = acc_x[:, 384:768].astype(BF)
    o_swap()
    lay_ref[...] = (block_f + fin[...].astype(F32)).astype(BF)

    for copy in copies.all:
        copy.wait_send()

    @pl.when(moves)
    def _():
        for copy in swaps:
            copy.wait_send()


def shards(inputs, qkv_weight, out_weight, up_weight, down_weight, grad_out):
    rows = qkv_weight.shape[0]
    vmem = pl.BlockSpec(memory_space=pltpu.VMEM)

    def buf(*shape, dtype=BF):
        return pltpu.VMEM(shape, dtype)

    layer_out, qkv_grad, out_grad, up_grad, down_grad = pl.pallas_call(
        kernel,
        out_shape=[
            jax.ShapeDtypeStruct(inputs.shape, BF),
            jax.ShapeDtypeStruct((3, rows, 128), BF),
            jax.ShapeDtypeStruct(out_weight.shape, BF),
            jax.ShapeDtypeStruct(up_weight.shape, BF),
            jax.ShapeDtypeStruct(down_weight.shape, BF),
        ],
        in_specs=[vmem] * 6,
        out_specs=[vmem] * 5,
        scratch_shapes=[
            buf(512, 512),
            buf(512, 384),
            buf(8, 8, TOK, dtype=F32),
            buf(8, TOK, 512),
            buf(2, 2, 8, TOK, 128),
            buf(2, 2, 8, TOK, 128),
            buf(10, 8, TOK, dtype=F32),
            buf(8, TOK, 512),
            buf(8, TOK, 384),
            buf(8, TOK, 384),
            buf(2, 2, TOK, 512),
            buf(2, 2, TOK, 384),
            buf(2, 2, TOK, 384),
            buf(2, 2, TOK // 2, 512),
            buf(2, 2, TOK // 2, 384),
            buf(2, 2, TOK // 2, 384),
            buf(TOK, 512),
            buf(TOK, 384),
            buf(TOK, 384),
            buf(TOK, 512),
            buf(TOK, 384),
            buf(TOK, 384),
            buf(8, TOK, 128),
            buf(8, TOK, 384),
            buf(8, TOK, 384),
            buf(8, TOK, 384),
            buf(2, 2, 8, TOK, 128),
            buf(2, 8, TOK, 128),
            buf(2, 8, TOK, 128),
            buf(3, 2, 2, TOK, 128),
            buf(2, 2, TOK, 128),
            buf(3, TOK, 128),
            buf(TOK, 128),
            buf(TOK, 128),
            buf(512, 768, dtype=F32),
            buf(512, 512, dtype=F32),
            pltpu.SemaphoreType.DMA((N_SEMS,)),
            pltpu.SemaphoreType.DMA((N_SEMS,)),
            pltpu.SemaphoreType.DMA((4,)),
        ],
        compiler_params=pltpu.CompilerParams(
            collective_id=0, has_side_effects=True, vmem_limit_bytes=56 * 2**20
        ),
    )(inputs, grad_out, jnp.transpose(qkv_weight, (1, 0, 2)), out_weight, up_weight, down_weight)
    return layer_out, jnp.transpose(qkv_grad, (1, 0, 2)), out_grad, up_grad, down_grad


def solution(mesh):
    placed = (
        P("dp", "mp"),
        P("dp", None, "mp"),
        P("mp", "dp"),
        P("dp", "mp"),
        P("mp", "dp"),
        P("dp", "mp"),
    )
    return jax.shard_map(
        shards,
        mesh=mesh,
        in_specs=placed,
        out_specs=(P("dp", "mp"), P("dp", None, "mp"), P("mp", "dp"), P("dp", "mp"), P("mp", "dp")),
        check_vma=False,
    )
```
